256 devices in a mesh: leaf: 64 (over y, z, core), panel: 4 (over x).
Axes of the slice: x: 4, y: 4, z: 8, core: 2. Of those that a mesh axis runs over, the one named last changes fastest.
Arguments:
- inverse_top: float32 [640, 640], P('leaf', 'panel'), may hold values from -1 to 2, as said below
- inverse_second: float32 [1280, 640], P('leaf', 'panel'), may hold values from -1 to 2, as said below
- inverse_third: float32 [2560, 640], P('leaf', 'panel'), may hold values from -1 to 2, as said below
- inverse_bottom: float32 [5120, 640], P('leaf', 'panel'), may hold values from -1 to 2, as said below
- below_second: float32 [1280, 640], P('leaf', 'panel'), may hold values from -0.125 to 0.125
- below_third: float32 [5120, 640], P('leaf', 'panel'), may hold values from -0.078125 to 0.078125
- below_bottom: float32 [15360, 640], P('leaf', 'panel'), may hold values from -0.0625 to 0.0625
Outputs:
- variance_top: float32 [640], P('leaf')
- variance_second: float32 [1280], P('leaf')
- variance_third: float32 [2560], P('leaf')
- variance_bottom: float32 [5120], P('leaf')
The draws below stay inside these ranges and needn't reach their ends.
Inputs may be any that keep to these rules, and one draw needn't show every extreme that they name: `inverse_top`: each aligned block of 640 rows is lower triangular, with its diagonal entries in 0.5 to 1.6. `inverse_second`: each aligned block of 640 rows is lower triangular, with its diagonal entries in 0.5 to 1.6. `inverse_third`: each aligned block of 640 rows is lower triangular, with its diagonal entries in 0.5 to 1.6. `inverse_bottom`: each aligned block of 640 rows is lower triangular, with its diagonal entries in 0.5 to 1.6.
All inputs are finite; a program needn't handle non-finite values.
Results may differ from the reference program's by a relative error of at most 0.00018.
Values sent between devices are 32-bit elements; how exact they have to be, the bound alone decides.
No kernel may reach another device: no remote copies, remote signals or barrier semaphores. Data moves between devices by JAX's collectives and lax.ppermute only.
A program may use at most 128 MiB of HBM per device.

```python
import math
import jax
import jax.numpy as jnp
from jax import lax

W = 640


def triangle(noise, diagonal):
    row_count = noise.shape[0]
    row_pos = (jnp.arange(row_count, dtype=jnp.int32) % W)[:, None]
    col_pos = jnp.arange(W, dtype=jnp.int32)[None, :]
    strict = jnp.where(col_pos < row_pos, noise * (0.5 / math.sqrt(W)), 0.0)
    return (strict + jnp.where(col_pos == row_pos, diagonal, 0.0)).astype(jnp.float32)


def draw_inverse_top(key, part):
    key = jax.random.fold_in(key, 11)
    noise_key, diag_key = jax.random.split(key)
    noise = jnp.clip(jax.random.normal(noise_key, (W, W), jnp.float32), -3.4, 3.4)
    diagonal = jax.random.uniform(diag_key, (W, 1), jnp.float32, 0.7, 1.3)
    return triangle(noise, diagonal)


def draw_inverse_second(key, part):
    key = jax.random.fold_in(key, 12)
    noise_key, diag_key = jax.random.split(key)
    noise = jnp.clip(jax.random.normal(noise_key, (2 * W, W), jnp.float32), -3.4, 3.4)
    diagonal = jax.random.uniform(diag_key, (2 * W, 1), jnp.float32, 0.7, 1.3)
    return triangle(noise, diagonal)


def draw_inverse_third(key, part):
    key = jax.random.fold_in(key, 13)
    noise_key, diag_key = jax.random.split(key)
    noise = jnp.clip(jax.random.normal(noise_key, (4 * W, W), jnp.float32), -3.4, 3.4)
    diagonal = jax.random.uniform(diag_key, (4 * W, 1), jnp.float32, 0.7, 1.3)
    return triangle(noise, diagonal)


def draw_inverse_bottom(key, part):
    key = jax.random.fold_in(key, 14)
    noise_key, diag_key = jax.random.split(key)
    noise = jnp.clip(jax.random.normal(noise_key, (8 * W, W), jnp.float32), -3.4, 3.4)
    diagonal = jax.random.uniform(diag_key, (8 * W, 1), jnp.float32, 0.7, 1.3)
    return triangle(noise, diagonal)


def steps_of(own_key, shape, shards, low, largest):
    def one(axis_at, blocks):
        steps = jax.random.uniform(jax.random.fold_in(jax.random.fold_in(own_key, 6), axis_at), (blocks,), jnp.float32, low / len(shards), largest / len(shards))
        return jnp.repeat(jnp.exp(steps), shape[axis_at] // blocks).reshape((-1,) + (1,) * (len(shape) - axis_at - 1))

    gain = one(*shards[0])
    for cut in shards[1:]:
        gain = gain * one(*cut)
    return gain


def bell_draw(key, extent, deviation, most, cuts=(), kind=jnp.bfloat16):
    array = deviation * jax.random.normal(key, extent, jnp.float32)
    if cuts:
        array = array * steps_of(key, extent, cuts, -0.22, 0.18)
    return jnp.clip(array, -most, most).astype(kind)


def setup_inputs(seed: int = 0) -> dict:
    streams_of = jax.random.split(jax.random.key(seed), 8)
    inverse_top = draw_inverse_top(jax.random.fold_in(streams_of[7], 71), 0)
    inverse_second = draw_inverse_second(jax.random.fold_in(streams_of[7], 71), 0)
    inverse_third = draw_inverse_third(jax.random.fold_in(streams_of[7], 71), 0)
    inverse_bottom = draw_inverse_bottom(jax.random.fold_in(streams_of[7], 71), 0)
    below_second = bell_draw(streams_of[4], (2 * W, W), (4 * W) ** -0.5, 0.125, ((0, 64), (1, 4)), jnp.float32)
    below_third = bell_draw(streams_of[5], (8 * W, W), (8 * W) ** -0.5, 0.078125, ((0, 64), (1, 4)), jnp.float32)
    below_bottom = bell_draw(streams_of[6], (24 * W, W), (12 * W) ** -0.5, 0.0625, ((0, 64), (1, 4)), jnp.float32)
    return {"inverse_top": inverse_top, "inverse_second": inverse_second, "inverse_third": inverse_third, "inverse_bottom": inverse_bottom, "below_second": below_second, "below_third": below_third, "below_bottom": below_bottom}


def batch_product(form, left_side, right_side):
    return jnp.einsum(form, left_side, right_side, precision=lax.Precision.HIGHEST)


def reference(inverse_top, inverse_second, inverse_third, inverse_bottom, below_second, below_third, below_bottom):
    inverses = [inverse_top, inverse_second, inverse_third, inverse_bottom]
    belows = [None, below_second, below_third, below_bottom]
    results = []
    path_block = None
    for height in range(4):
        node_count = 2 ** height
        inverse = inverses[height].reshape(node_count, W, W)
        if height == 0:
            gram_block = batch_product("kjc,kjd->kcd", inverse, inverse)
            results.append(jnp.diagonal(gram_block, axis1=1, axis2=2).reshape(node_count * W))
            path_block = gram_block
        else:
            below_block = belows[height].reshape(node_count, height * W, W)
            mixed_block = batch_product("krj,kjc->krc", below_block, inverse)
            side_block = -batch_product("krs,ksc->krc", path_block, mixed_block)
            if height < 3:
                gram_block = batch_product("kjc,kjd->kcd", inverse, inverse) - batch_product("krc,krd->kcd", mixed_block, side_block)
                results.append(jnp.diagonal(gram_block, axis1=1, axis2=2).reshape(node_count * W))
                upper_half = jnp.concatenate([path_block, side_block], 2)
                lower_half = jnp.concatenate([jnp.transpose(side_block, (0, 2, 1)), gram_block], 2)
                path_block = jnp.concatenate([upper_half, lower_half], 1)
            else:
                variance = jnp.sum(inverse * inverse, 1) - jnp.sum(mixed_block * side_block, 1)
                results.append(variance.reshape(node_count * W))
        if height < 3:
            path_block = jnp.repeat(path_block, 2, axis=0)
    return (results[0], results[1], results[2], results[3])
```

```python
import functools

import jax
import jax.numpy as jnp
import numpy as np
from jax import lax
from jax.experimental import pallas as pl
from jax.experimental.pallas import tpu as pltpu
from jax.sharding import Mesh
from jax.sharding import PartitionSpec as P

W = 640
Q = 160
ALL = ("node", "lane", "panel")
F32 = jnp.float32
VMEM = pl.BlockSpec(memory_space=pltpu.VMEM)
SMEM = pl.BlockSpec(memory_space=pltpu.SMEM)
HBM = pl.BlockSpec(memory_space=pl.ANY)


def device(y, z, c, x):
    return ((y % 4 * 8 + z % 8) * 2 + c) * 4 + x % 4


def pairs_of(move):
    pairs = []
    for y in range(4):
        for z in range(8):
            for c in range(2):
                for x in range(4):
                    pairs.append((device(y, z, c, x), device(*move(y, z, c, x))))
    return pairs


def step_x(parity):
    return pairs_of(lambda y, z, c, x: (y, z, c, x + (1 if (x + c + parity) % 2 == 0 else -1)))


def step_z(parity):
    return pairs_of(lambda y, z, c, x: (y, z + (1 if (z + c + parity) % 2 == 0 else -1), c, x))


def step_y(count):
    return pairs_of(lambda y, z, c, x: (y + count, z, c, x))


SWAP = pairs_of(lambda y, z, c, x: (y, z, 1 - c, x))


def to_owner(y, z, c, x):
    lane = z % 4 * 2 + c
    lane, x = 2 * x + lane // 4, lane % 4
    return (y, z // 4 * 4 + lane // 2, lane % 2, x)


OWNER = pairs_of(to_owner)


def permute(value, pairs):
    return lax.ppermute(value, ALL, pairs)


def permute_ids(ids, pairs):
    moved = np.zeros_like(ids)
    for source, target in pairs:
        moved[target] = ids[source]
    return moved


def gather_x(chunk, move, join):
    pair = join(chunk, move(chunk, step_x(0)))
    return [pair, move(pair, step_x(1))]


def gather_z(chunk, move, join):
    pair = join(chunk, move(chunk, step_z(0)))
    second = move(pair, step_z(1))
    third = move(second, step_z(0))
    return [pair, second, third, move(third, step_z(1))]


def join_rows(first, second):
    return jnp.concatenate([first, second], 0)


def join_ids(first, second):
    return np.concatenate([first, second], 1)


def natural_ids():
    ids = np.zeros((256, 1), np.int32)
    for y in range(4):
        for z in range(8):
            for c in range(2):
                for x in range(4):
                    ids[device(y, z, c, x), 0] = (z * 2 + c) * 4 + x
    return ids


def id_tables():
    own = natural_ids()
    by_x = join_ids(*gather_x(own, permute_ids, join_ids))
    first = gather_z(by_x, permute_ids, join_ids)
    first = first + [permute_ids(part, SWAP) for part in first]
    by_z = functools.reduce(join_ids, gather_z(own, permute_ids, join_ids))
    second = gather_x(by_z, permute_ids, join_ids)
    second = second + [permute_ids(part, SWAP) for part in second]
    return (
        by_x % 4,
        functools.reduce(join_ids, first),
        functools.reduce(join_ids, second),
    )


def split(value):
    high = value.astype(jnp.bfloat16)
    return high, (value - high.astype(F32)).astype(jnp.bfloat16)


def dot(left, right):
    return jnp.dot(left, right, preferred_element_type=F32)


def split_dot(left, right):
    rows = left.shape[0]
    left_high, left_low = split(left)
    right_high, right_low = split(right)
    both = dot(jnp.concatenate([left_high, left_low], 0), right_high)
    return both[:rows] + both[rows:] + dot(left_high, right_low)


def place(pieces, width):
    rows = pieces[0][0].shape[0]
    lane = lax.broadcasted_iota(jnp.int32, (rows, 128), 1)
    tiles = []
    for tile in range(width // 128):
        low = tile * 128
        total = jnp.zeros((rows, 128), F32)
        for value, source, length, target in pieces:
            start, stop = max(target, low), min(target + length, low + 128)
            if start >= stop:
                continue
            shift = (target - source) % 128
            moved = pltpu.roll(value, shift, 1) if shift else value
            inside = (lane >= start - low) & (lane < stop - low)
            total = jnp.where(inside, moved, total)
        tiles.append(total)
    return jnp.concatenate(tiles, 1)


def pack_kernel(d2, b2, b3, d1, b1, d0, x_out, y_out, rows):
    rows[...] = jnp.zeros(rows.shape, F32)
    rows[0:40, 0:Q] = d2[...]
    rows[40:120, 0:Q] = b2[...]
    x_out[0:Q, :] = rows[0:128, :].T[:Q]
    rows[0:240, 0:Q] = b3[...]
    below = rows[...].T
    x_out[Q : 2 * Q, :] = below[:Q, 0:128]
    x_out[2 * Q : 3 * Q, :] = below[:Q, 128:256]
    rows[0:128, :] = jnp.zeros((128, 256), F32)
    rows[0:20, 0:Q] = d1[...]
    rows[20:40, 0:Q] = b1[...]
    rows[40:50, 0:Q] = d0[...]
    y_out[...] = rows[0:128, :].T[:Q]


def merge_kernel(odd, own, one, two, three, out):
    lane = lax.broadcasted_iota(jnp.int32, (Q, 128), 1)
    is_odd = odd[0] == 1
    lower = jnp.where(is_odd, one[...], own[...])
    upper = jnp.where(is_odd, own[...], three[...])
    total = jnp.zeros((Q, 128), F32)
    for value, shift, start, stop in (
        (lower, 0, 0, 20),
        (upper, 20, 20, 40),
        (lower, 20, 40, 60),
        (upper, 40, 60, 80),
        (own[...], 40, 80, 90),
        (one[...], 50, 90, 100),
        (two[...], 60, 100, 110),
        (three[...], 70, 110, 120),
    ):
        moved = pltpu.roll(value, shift, 1) if shift else value
        total = jnp.where((lane >= start) & (lane < stop), moved, total)
    out[...] = total


def bottom_kernel(slots, inverse, pair, other, out, below, wide, sems):
    copies = []
    for slot in range(4):
        source = pair if slot < 2 else other
        column = pl.multiple_of(slots[slot] * Q, Q)
        for half in range(2):
            start = slot % 2 * 3 * Q + (1 + half) * Q
            copies.append(
                pltpu.make_async_copy(
                    source.at[pl.ds(start, Q), :],
                    below.at[half, pl.ds(column, Q), :],
                    sems.at[slot * 2 + half],
                )
            )
    for copy in copies:
        copy.start()
    wide[...] = jnp.zeros(wide.shape, F32)
    wide[:, 0:Q] = inverse[...]
    turned = wide[...].T[:Q]
    squares = jnp.sum(turned * turned, 1, keepdims=True)
    for copy in copies:
        copy.wait()
    mixed = split_dot(turned, jnp.concatenate([below[0], below[1]], 1))
    lane = lax.broadcasted_iota(jnp.int32, (Q, 256), 1)
    mixed = jnp.where(lane == 240, squares, mixed)
    out[...] = jnp.zeros(out.shape, F32)
    for part in range(8):
        out[part, 0:20, :] = mixed[part * 20 : part * 20 + 20]


def start_copies(table, sources, stage, sems):
    each = 64 // len(sources)
    copies = []
    for index, source in enumerate(sources):
        for atom in range(each):
            number = index * each + atom
            row = pl.multiple_of(table[number] * Q, Q)
            copies.append(
                pltpu.make_async_copy(
                    source.at[pl.ds(atom * Q, Q), :], stage.at[pl.ds(row, Q), :], sems.at[number]
                )
            )
    for copy in copies:
        copy.start()
    return copies


def block(stage, z):
    return jnp.concatenate(
        [stage[(2 * z) * W : (2 * z + 1) * W, :], stage[(2 * z + 1) * W : (2 * z + 2) * W, :]], 1
    )


def one_hot(rows, count, base):
    row = lax.broadcasted_iota(jnp.int32, (rows, W), 0)
    lane = lax.broadcasted_iota(jnp.int32, (rows, W), 1)
    return jnp.where((row < count) & (lane == base + row), 1.0, 0.0).astype(F32)


def third_kernel(table, base, mixed, *refs):
    sources = refs[:8]
    out, squares_out, stage, sems = refs[8:]
    copies = start_copies(table, sources, stage, sems)
    pieces = []
    for part in range(8):
        pieces.append((mixed[part, :, 0:128], 0, 128, part * 240))
        pieces.append((mixed[part, :, 128:256], 0, 112, part * 240 + 128))
    path = place(pieces, 3 * W)
    squares = mixed[0, :, 240:241]
    for copy in copies:
        copy.wait()
    cols = jnp.concatenate([path[:, 2 * W :], one_hot(16, 10, base[0])], 0)
    pieces = []
    for z in range(8):
        product = split_dot(cols, block(stage, z))
        for core in range(2):
            piece = product[:, core * 128 : core * 128 + 128]
            pieces.append((piece, 0, 40, z * 80 + core * 40))
    cols = place(pieces, W)
    squares = jnp.concatenate([squares, jnp.zeros((16, 1), F32)], 0)
    squares = squares + jnp.sum(cols * cols, 1, keepdims=True)
    pieces = []
    for z in range(8):
        product = split_dot(cols, block(stage, z))
        for core in range(2):
            piece = product[:, core * 128 : core * 128 + 128]
            pieces.append((piece, 40, 80, z * 160 + core * 80))
    change = place(pieces, 2 * W)
    out[0:24, :] = path[:, : 2 * W] - change[0:24]
    out[24:40, :] = -change[24:40]
    squares_out[...] = jnp.broadcast_to(squares, (40, 128))


def top_kernel(table, base, path, squares_in, *refs):
    sources = refs[:4]
    out, stage, sems = refs[4:]
    copies = start_copies(table, sources, stage, sems)
    for copy in copies:
        copy.wait()
    cols = jnp.concatenate([path[:, W:], one_hot(8, 5, base[1])], 0)
    pieces = []
    for z in range(8):
        product = split_dot(cols, block(stage, z))
        for core in range(2):
            piece = product[:, core * 128 : core * 128 + 128]
            for half in range(2):
                pieces.append((piece, half * 20, 20, half * 320 + z * 40 + core * 20))
    cols = place(pieces, W)
    squares = jnp.concatenate([squares_in[:, 0:1], jnp.zeros((8, 1), F32)], 0)
    squares = squares + jnp.sum(cols * cols, 1, keepdims=True)
    pieces = []
    for z in range(8):
        product = split_dot(cols, block(stage, z))
        for core in range(2):
            piece = product[:, core * 128 : core * 128 + 128]
            for half in range(2):
                pieces.append((piece, 40 + half * 20, 20, half * 320 + z * 40 + core * 20))
    change = place(pieces, W)
    cols = jnp.concatenate(
        [path[:, :W] - change[0:40], -change[40:48], one_hot(16, 10, base[2])], 0
    )
    squares = jnp.concatenate([squares, jnp.zeros((16, 1), F32)], 0)
    lane = lax.broadcasted_iota(jnp.int32, (64, 256), 1) % 128
    used = (lane >= 80) & (lane < 120)
    total = jnp.zeros((64, 256), F32)
    for z in range(8):
        product = split_dot(cols, block(stage, z))
        total = total + jnp.where(used, product * product, 0.0)
    squares = squares + jnp.sum(total, 1, keepdims=True)
    square = jnp.concatenate(
        [jnp.broadcast_to(squares, (64, 128)), jnp.zeros((64, 128), F32)], 0
    )
    out[...] = square.T[0:1, :]


def call(kernel, out_shapes, in_specs, scratch=(), flops=0, moved=0):
    shapes = [jax.ShapeDtypeStruct(shape, F32) for shape in out_shapes]
    return pl.pallas_call(
        kernel,
        out_shape=shapes,
        in_specs=in_specs,
        out_specs=[VMEM] * len(shapes),
        scratch_shapes=list(scratch),
        compiler_params=pltpu.CompilerParams(vmem_limit_bytes=40 * 2**20),
        cost_estimate=pl.CostEstimate(flops=flops, bytes_accessed=moved, transcendentals=0),
    )


def shards(d0, d1, d2, d3, b1, b2, b3):
    leaf = lax.axis_index("node") * 8 + lax.axis_index("lane")
    panel = lax.axis_index("panel")
    own = leaf * 4 + panel
    slots, first_table, second_table = [
        lax.dynamic_index_in_dim(jnp.asarray(table), own, 0, keepdims=False)
        for table in id_tables()
    ]
    base = jnp.stack(
        [leaf % 16 * 40 + panel * 10, leaf % 32 * 20 + panel * 5, leaf * 10]
    ).astype(jnp.int32)
    odd = (leaf // 16 % 2).astype(jnp.int32).reshape(1)

    x_chunk, y_chunk = call(
        pack_kernel,
        [(3 * Q, 128), (Q, 128)],
        [VMEM] * 6,
        [pltpu.VMEM((256, 256), F32)],
        moved=600000,
    )(d2, b2, b3, d1, b1, d0)

    x_parts = gather_x(x_chunk, permute, join_rows)
    others = [permute(y_chunk, step_y(count)) for count in (1, 2, 3)]
    (top_chunk,) = call(merge_kernel, [(Q, 128)], [SMEM] + [VMEM] * 4, moved=400000)(
        odd, y_chunk, *others
    )
    z_chunk = jnp.concatenate(
        [part[start : start + Q] for part in x_parts for start in (0, 3 * Q)], 0
    )
    third_parts = gather_z(z_chunk, permute, join_rows)
    third_parts = third_parts + [permute(part, SWAP) for part in third_parts]
    top_rows = functools.reduce(join_rows, gather_z(top_chunk, permute, join_rows))
    top_parts = gather_x(top_rows, permute, join_rows)
    top_parts = top_parts + [permute(part, SWAP) for part in top_parts]

    inverse = lax.all_gather(d3, "lane", axis=0, tiled=True)
    (mixed,) = call(
        bottom_kernel,
        [(8, 24, 256)],
        [SMEM, VMEM, HBM, HBM],
        [
            pltpu.VMEM((2, W, 128), F32),
            pltpu.VMEM((W, 256), F32),
            pltpu.SemaphoreType.DMA((8,)),
        ],
        flops=2 * 3 * W * 256 * 256,
        moved=2000000,
    )(slots, inverse, *x_parts)
    mixed = lax.all_to_all(mixed, "lane", 0, 0, tiled=True)
    mixed = permute(mixed, OWNER)

    stage = [pltpu.VMEM((16 * W, 128), F32), pltpu.SemaphoreType.DMA((64,))]
    path, squares = call(
        third_kernel,
        [(40, 2 * W), (40, 128)],
        [SMEM, SMEM, VMEM] + [HBM] * 8,
        stage,
        flops=2 * 6 * 40 * W * 16 * 128,
        moved=6000000,
    )(first_table, base, mixed, *third_parts)
    (variances,) = call(
        top_kernel,
        [(1, 128)],
        [SMEM, SMEM, VMEM, VMEM] + [HBM] * 4,
        stage,
        flops=2 * 9 * 48 * W * 16 * 128,
        moved=6000000,
    )(second_table, base, path, squares, *top_parts)
    gathered = lax.all_gather(variances, "panel", axis=0, tiled=True)
    return (
        variances[0, 48:58],
        gathered[:, 40:45].reshape(20),
        gathered[:, 24:34].reshape(40),
        gathered[:, 0:20].reshape(80),
    )


def solution(mesh):
    fine = Mesh(mesh.devices.reshape(8, 8, 4), ALL)
    rows = ("node", "lane")
    return jax.shard_map(
        shards,
        mesh=fine,
        in_specs=(P(rows, "panel"),) * 7,
        out_specs=(P(rows),) * 4,
        check_vma=False,
    )
```

```python
import jax
import jax.numpy as jnp
from jax import lax
from jax.experimental import pallas as pl
from jax.experimental.pallas import tpu as pltpu
from jax.sharding import Mesh
from jax.sharding import PartitionSpec as P

W = 640
Q = 160
ALL = ("row", "high", "deep", "core", "panel")
F32 = jnp.float32
VMEM = pl.BlockSpec(memory_space=pltpu.VMEM)
HBM = pl.BlockSpec(memory_space=pl.ANY)


def device(y, z, c, x):
    return ((y % 4 * 8 + z % 8) * 2 + c) * 4 + x % 4


def pairs_of(move):
    pairs = []
    for y in range(4):
        for z in range(8):
            for c in range(2):
                for x in range(4):
                    pairs.append((device(y, z, c, x), device(*move(y, z, c, x))))
    return pairs


def step_x(parity):
    return pairs_of(lambda y, z, c, x: (y, z, c, x + (1 if (x + c + parity) % 2 == 0 else -1)))


def step_z(parity):
    return pairs_of(lambda y, z, c, x: (y, z + (1 if (z + c + parity) % 2 == 0 else -1), c, x))


def step_y(count):
    return pairs_of(lambda y, z, c, x: (y + count, z, c, x))


def step_near(mask):
    return pairs_of(lambda y, z, c, x: (y, z ^ mask, c, x))


SWAP = pairs_of(lambda y, z, c, x: (y, z, 1 - c, x))


ORDER = (0, 1, -1, -2, 2, 3, -3, -4)


def join(first, second):
    return jnp.concatenate([first, second], 0)


def tie(value, *others):
    return lax.optimization_barrier((value, *others))[0]


def permute(value, pairs, name):
    with jax.named_scope(name):
        return lax.ppermute(value, ALL, pairs)


def here():
    depth = lax.axis_index("high") * 4 + lax.axis_index("deep")
    return lax.axis_index("row"), depth, lax.axis_index("core"), lax.axis_index("panel")


def turn(place, core):
    return 1 - 2 * ((place + core) & 1)


def third_rows(z, c, x):
    panels = [(x + turn(x, c) * step & 3) + c * 4 for step in (0, 1, -1, -2)]
    depths = [(z + turn(z, c) * step & 7) * 8 for step in ORDER]
    return [depth + panel for panel in panels for depth in depths]


def top_rows(z, c, x):
    panels = [(x + turn(x, c) * step & 3) + c * 4 for step in (0, 1, -1, -2)]
    depths = [(z + turn(z, c) * step & 7) * 8 for step in ORDER]
    return [depth + panel for depth in depths for panel in panels]


def split(value):
    high = value.astype(jnp.bfloat16)
    return high, (value - high.astype(F32)).astype(jnp.bfloat16)


def dot(left, right):
    return jnp.dot(left, right, preferred_element_type=F32)


def split_dot(left, right):
    rows = left.shape[0]
    left_high, left_low = split(left)
    right_high, right_low = split(right)
    both = dot(jnp.concatenate([left_high, left_low], 0), right_high)
    return both[:rows] + both[rows:] + dot(left_high, right_low)


def place(pieces, width):
    rows = pieces[0][0].shape[0]
    lane = lax.broadcasted_iota(jnp.int32, (rows, 128), 1)
    tiles = []
    for tile in range(width // 128):
        low = tile * 128
        total = jnp.zeros((rows, 128), F32)
        for value, source, length, target in pieces:
            start, stop = max(target, low), min(target + length, low + 128)
            if start >= stop:
                continue
            shift = (target - source) % 128
            moved = pltpu.roll(value, shift, 1) if shift else value
            inside = (lane >= start - low) & (lane < stop - low)
            total = jnp.where(inside, moved, total)
        tiles.append(total)
    return jnp.concatenate(tiles, 1)


def pack_kernel(d2, b2, b3, d3, d1, b1, d0, y_out, h_out, b_out, h2, g2, g3, h3, h1, g1, h0, rows, sems):
    copies = [
        pltpu.make_async_copy(source, target, sems.at[index])
        for index, (source, target) in enumerate(
            [(d1, h1), (b1, g1), (d0, h0), (d2, h2), (b2, g2), (b3, g3), (d3, h3)]
        )
    ]
    for copy in copies:
        copy.start()
    rows[...] = jnp.zeros(rows.shape, F32)
    b_out[...] = jnp.zeros(b_out.shape, F32)
    for copy in copies:
        copy.wait()
    rows[0:20, 0:Q] = h1[...]
    rows[20:40, 0:Q] = g1[...]
    rows[40:50, 0:Q] = h0[...]
    y_out[...] = rows[...].T[:Q]
    rows[0:40, 0:Q] = h2[...]
    rows[40:120, 0:Q] = g2[...]
    h_out[...] = rows[...].T[:Q]
    b_out[0:Q, :] = g3[:, 0:128]
    b_out[Q : 2 * Q, 0:112] = g3[:, 128:240]
    rows[0:80, 0:Q] = h3[...]
    rows[80:128, :] = jnp.zeros((48, 256), F32)
    turned = rows[...].T[:Q]
    for panel in range(4):
        for half in range(2):
            target = 2 * Q + panel * 40 + half * 20
            source = half * 80 + panel * 20
            b_out[target : target + 20, :] = turned[source : source + 20]


def merge_kernel(own, one, two, three, out):
    lane = lax.broadcasted_iota(jnp.int32, (Q, 128), 1)
    is_odd = here()[0] & 1 == 1
    lower = jnp.where(is_odd, one[...], own[...])
    upper = jnp.where(is_odd, own[...], three[...])
    total = jnp.zeros((Q, 128), F32)
    for value, shift, start, stop in (
        (lower, 0, 0, 20),
        (upper, 20, 20, 40),
        (lower, 20, 40, 60),
        (upper, 40, 60, 80),
        (own[...], 40, 80, 90),
        (one[...], 50, 90, 100),
        (two[...], 60, 100, 110),
        (three[...], 70, 110, 120),
    ):
        moved = pltpu.roll(value, shift, 1) if shift else value
        total = jnp.where((lane >= start) & (lane < stop), moved, total)
    out[...] = total


def b_panels():
    _, _, c, x = here()
    return [x + turn(x, c) * ORDER[slot] & 3 for slot in range(4)]


def run(copies, sems):
    copies = [
        pltpu.make_async_copy(source, target, sems.at[index])
        for index, (source, target) in enumerate(copies)
    ]
    for copy in copies:
        copy.start()
    for copy in copies:
        copy.wait()


def pick_kernel(pair, last, out, sems):
    _, _, _, x = here()
    copies = []
    for slot, panel in enumerate(b_panels()):
        source = pair if slot < 2 else last
        start = pl.multiple_of(slot % 2 * 3 * Q + 2 * Q + x * 40, 8)
        target = pl.multiple_of(panel * 40, 8)
        copies.append((source.at[pl.ds(start, 40), :], out.at[pl.ds(target, 40), :]))
    run(copies, sems)


def bottom_kernel(near, near_other, pair, last, out, below, inverse, sems):
    _, z, c, x = here()
    copies = []
    for slot, panel in enumerate(b_panels()):
        source = pair if slot < 2 else last
        column = pl.multiple_of(panel * Q, Q)
        for half in range(2):
            start = slot % 2 * 3 * Q + half * Q
            copies.append((source.at[pl.ds(start, Q), :], below.at[half, pl.ds(column, Q), :]))
    for core, source in enumerate((near, near_other)):
        for slot in range(4):
            lane = (z & 3 ^ slot) * 2 + (c ^ core)
            copies.append((source.at[pl.ds(slot * Q, Q), :], inverse.at[lane]))
    run(copies, sems)
    squares = jnp.zeros((Q, 128), F32)
    mixed = jnp.zeros((Q, 256), F32)
    for lane in range(8):
        part = inverse[lane]
        squares = squares + part * part
        rows = slice(lane * 80, lane * 80 + 80)
        mixed = mixed + split_dot(
            part[:, :80], jnp.concatenate([below[0, rows, :], below[1, rows, :]], 1)
        )
    squares = jnp.sum(squares, 1, keepdims=True)
    lane = lax.broadcasted_iota(jnp.int32, (Q, 256), 1)
    mixed = jnp.where(lane == 240, squares, mixed)
    out[...] = jnp.zeros(out.shape, F32)
    for part in range(8):
        out[part, 0:20, :] = mixed[part * 20 : part * 20 + 20]


def start_copies(sources, rows, stage, sems):
    each = 64 // len(sources)
    copies = []
    for number, row in enumerate(rows):
        source, atom = sources[number // each], number % each
        row = pl.multiple_of(row * Q, Q)
        copies.append(
            pltpu.make_async_copy(
                source.at[pl.ds(atom * Q, Q), :], stage.at[pl.ds(row, Q), :], sems.at[number]
            )
        )
    for copy in copies:
        copy.start()
    return copies


def split_stage(stage, high, low):
    for z in range(8):
        for core in range(2):
            rows = slice((2 * z + core) * W, (2 * z + core + 1) * W)
            lanes = slice(core * 128, core * 128 + 128)
            high[z, :, lanes], low[z, :, lanes] = split(stage[rows, :])


def halves(left):
    left_high, left_low = split(left)
    return left_high, jnp.concatenate([left_high, left_low], 0)


def half_dot(left, high, low):
    left_high, left_both = left
    rows = left_high.shape[0]
    both = dot(left_both, high)
    return both[:rows] + both[rows:] + dot(left_high, low)


def one_hot(rows, count, base):
    row = lax.broadcasted_iota(jnp.int32, (rows, W), 0)
    lane = lax.broadcasted_iota(jnp.int32, (rows, W), 1)
    return jnp.where((row < count) & (lane == base + row), 1.0, 0.0).astype(F32)


def chain_kernel(mixed, *refs):
    first, second, third, last = refs[8:12]
    h_parts = [(second, 1), (third, 1), (third, 2), (last, 1)]
    t_parts = [(first, 0), (second, 0), (third, 0), (last, 0)]
    rows = 8 * Q
    third = refs[:4] + tuple(swap.at[pl.ds(part * rows, rows), :] for swap, part in h_parts)
    top = refs[4:8] + tuple(swap.at[pl.ds(part * rows, rows), :] for swap, part in t_parts)
    out, third_stage, top_stage, high, low, third_sems, top_sems = refs[12:]
    y, z, c, x = here()
    leaf = z * 2 + c
    third_copies = start_copies(
        third, third_rows(z, c, x) + third_rows(z, 1 - c, x), third_stage, third_sems
    )
    top_copies = start_copies(
        top, top_rows(z, c, x) + top_rows(z, 1 - c, x), top_stage, top_sems
    )
    pieces = []
    for part in range(8):
        pieces.append((mixed[part, :, 0:128], 0, 128, part * 240))
        pieces.append((mixed[part, :, 128:256], 0, 112, part * 240 + 128))
    path = place(pieces, 3 * W)
    squares = jnp.concatenate([mixed[0, :, 240:241], jnp.zeros((40, 1), F32)], 0)

    def products(cols):
        left = halves(cols)
        for z in range(8):
            product = half_dot(left, high[z], low[z])
            for core in range(2):
                yield z, core, product[:, core * 128 : core * 128 + 128]

    for copy in third_copies:
        copy.wait()
    split_stage(third_stage, high, low)
    cols = jnp.concatenate([path[:, 2 * W :], one_hot(16, 10, leaf * 40 + x * 10)], 0)
    pieces = [(part, 0, 40, z * 80 + core * 40) for z, core, part in products(cols)]
    cols = place(pieces, W)
    squares = squares + jnp.concatenate(
        [jnp.sum(cols * cols, 1, keepdims=True), jnp.zeros((24, 1), F32)], 0
    )
    pieces = [(part, 40, 80, z * 160 + core * 80) for z, core, part in products(cols)]
    change = place(pieces, 2 * W)
    path = jnp.concatenate([path[:, : 2 * W] - change[0:24], -change[24:40]], 0)

    for copy in top_copies:
        copy.wait()
    split_stage(top_stage, high, low)
    cols = jnp.concatenate([path[:, W:], one_hot(8, 5, ((y & 1) * 16 + leaf) * 20 + x * 5)], 0)
    pieces = [
        (part, half * 20, 20, half * 320 + z * 40 + core * 20)
        for z, core, part in products(cols)
        for half in range(2)
    ]
    cols = place(pieces, W)
    squares = squares + jnp.concatenate(
        [jnp.sum(cols * cols, 1, keepdims=True), jnp.zeros((16, 1), F32)], 0
    )
    pieces = [
        (part, 40 + half * 20, 20, half * 320 + z * 40 + core * 20)
        for z, core, part in products(cols)
        for half in range(2)
    ]
    change = place(pieces, W)
    cols = jnp.concatenate(
        [path[:, :W] - change[0:40], -change[40:48], one_hot(16, 10, (y * 16 + leaf) * 10)], 0
    )
    lane = lax.broadcasted_iota(jnp.int32, (64, 128), 1)
    total = jnp.zeros((64, 128), F32)
    for _, _, part in products(cols):
        total = total + part * part
    total = jnp.where((lane >= 80) & (lane < 120), total, 0.0)
    squares = squares + jnp.sum(total, 1, keepdims=True)
    square = jnp.concatenate(
        [jnp.broadcast_to(squares, (64, 128)), jnp.zeros((64, 128), F32)], 0
    )
    out[...] = square.T[0:1, :]


def finish_kernel(own, gathered, *outs):
    for out, start, count in zip(outs, (48, 40, 24, 0), (10, 5, 10, 20)):
        if start == 48:
            out[...] = own[0:1, start : start + count]
            continue
        parts = []
        for panel in range(4):
            row = jnp.broadcast_to(gathered[panel : panel + 1, :], (8, 128))
            parts.append((row, start, count, panel * count))
        out[...] = place(parts, 128)[0:1, : 4 * count]


def call(kernel, out_shapes, in_specs, scratch=(), limit=24):
    shapes = [jax.ShapeDtypeStruct(shape, F32) for shape in out_shapes]
    return pl.pallas_call(
        kernel,
        out_shape=shapes,
        in_specs=in_specs,
        out_specs=[VMEM] * len(shapes),
        scratch_shapes=list(scratch),
        compiler_params=pltpu.CompilerParams(vmem_limit_bytes=limit * 2**20),
        cost_estimate=pl.CostEstimate(flops=0, bytes_accessed=0, transcendentals=0),
    )


def shards(d0, d1, d2, d3, b1, b2, b3):
    b3 = b3.T
    y_chunk, h_chunk, b_chunk = call(
        pack_kernel,
        [(Q, 128), (Q, 128), (3 * Q, 128)],
        [HBM] * 7,
        [pltpu.VMEM(value.shape, F32) for value in (d2, b2, b3, d3, d1, b1, d0)]
        + [pltpu.VMEM((128, 256), F32), pltpu.SemaphoreType.DMA((7,))],
        limit=60,
    )(d2, b2, b3, d3, d1, b1, d0)

    def send(name, pairs, value):
        return permute(value, pairs, name)

    def together(*values):
        return lax.optimization_barrier(values)

    y1 = send("y1", step_y(1), y_chunk)
    y3 = send("y3", step_y(3), y_chunk)
    y2 = send("y2", step_y(2), y_chunk)
    hz = send("hz0", step_z(0), h_chunk)
    bx = send("bx0", step_x(0), b_chunk)
    y1, y2, y3, hz, bx = together(y1, y2, y3, hz, bx)
    (t_chunk,) = call(merge_kernel, [(Q, 128)], [VMEM] * 4)(y_chunk, y1, y2, y3)
    h_pair, b_pair = join(h_chunk, hz), join(b_chunk, bx)
    t_chunk, h_pair, b_pair = together(t_chunk, h_pair, b_pair)

    tx = send("tx0", step_x(0), t_chunk)
    h1 = send("hz1", step_z(1), h_pair)
    b_last = send("bx1", step_x(1), b_pair)
    tx, h1, b_last = together(tx, h1, b_last)
    t_pair = join(t_chunk, tx)
    (near,) = call(
        pick_kernel, [(Q, 128)], [HBM] * 2, [pltpu.SemaphoreType.DMA((4,))]
    )(b_pair, b_last)
    t_pair, h1, near = together(t_pair, h1, near)

    tx = send("tx1", step_x(1), t_pair)
    h2 = send("hz2", step_z(0), h1)
    got = send("near1", step_near(1), near)
    tx, h2, got = together(tx, h2, got)
    t_line, near = join(t_pair, tx), join(near, got)
    t_line, near, h2 = together(t_line, near, h2)

    tz = send("tz0", step_z(0), t_line)
    h3 = send("hz3", step_z(1), h2)
    got = send("near2", step_near(2), near)
    tz, h3, got = together(tz, h3, got)
    t0, near = join(t_line, tz), join(near, got)
    h_rows = jnp.concatenate([h_pair, h1, h2, h3], 0)
    t0, h_rows, near = together(t0, h_rows, near)

    t1 = send("tz1", step_z(1), t0)
    hx = send("hx0", step_x(0), h_rows)
    near_other = send("near_swap", SWAP, near)
    swap0 = send("swap0", SWAP, t0)
    t1, hx, near_other, swap0, h_rows = together(t1, hx, near_other, swap0, h_rows)

    t2 = send("tz2", step_z(0), t1)
    h1 = send("hx1", step_x(1), h_rows)
    swap1 = send("swap1", SWAP, join(t1, h_rows))
    (mixed,) = call(
        bottom_kernel,
        [(8, 24, 256)],
        [HBM] * 4,
        [
            pltpu.VMEM((2, W, 128), F32),
            pltpu.VMEM((8, Q, 128), F32),
            pltpu.SemaphoreType.DMA((16,)),
        ],
    )(near, near_other, b_pair, b_last)
    t2, h1, swap1, mixed, hx = together(t2, h1, swap1, mixed, hx)

    t3 = send("tz3", step_z(1), t2)
    h2 = send("hx2", step_x(1), hx)
    swap2 = send("swap2", SWAP, jnp.concatenate([t2, hx, h1], 0))
    mixed = lax.all_to_all(mixed, ("deep", "core"), 0, 0, tiled=True)
    t3, h2, mixed, swap2 = together(t3, h2, mixed, swap2)

    swap3 = send("swap3", SWAP, join(t3, h2))

    (variances,) = call(
        chain_kernel,
        [(1, 128)],
        [VMEM] + [HBM] * 12,
        [
            pltpu.VMEM((16 * W, 128), F32),
            pltpu.VMEM((16 * W, 128), F32),
            pltpu.VMEM((8, W, 256), jnp.bfloat16),
            pltpu.VMEM((8, W, 256), jnp.bfloat16),
            pltpu.SemaphoreType.DMA((64,)),
            pltpu.SemaphoreType.DMA((64,)),
        ],
        limit=60,
    )(mixed, h_rows, hx, h1, h2, t0, t1, t2, t3, swap0, swap1, swap2, swap3)
    gathered = lax.all_gather(variances, "panel", axis=0, tiled=True)
    outs = call(finish_kernel, [(1, 10), (1, 20), (1, 40), (1, 80)], [VMEM] * 2)(
        variances, gathered
    )
    return tuple(out.reshape(out.shape[1]) for out in outs)


def solution(mesh):
    fine = Mesh(mesh.devices.reshape(4, 2, 4, 2, 4), ALL)
    rows = ALL[:4]
    return jax.shard_map(
        shards,
        mesh=fine,
        in_specs=(P(rows, "panel"),) * 7,
        out_specs=(P(rows),) * 4,
        check_vma=False,
    )
```

```python
import jax
import jax.numpy as jnp
from jax import lax
from jax.experimental import pallas as pl
from jax.experimental.pallas import tpu as pltpu
from jax.sharding import Mesh
from jax.sharding import PartitionSpec as P

W = 640
Q = 160
ALL = ("row", "high", "deep", "core", "panel")
F32 = jnp.float32
VMEM = pl.BlockSpec(memory_space=pltpu.VMEM)
HBM = pl.BlockSpec(memory_space=pl.ANY)


def device(y, z, c, x):
    return ((y % 4 * 8 + z % 8) * 2 + c) * 4 + x % 4


def pairs_of(move):
    pairs = []
    for y in range(4):
        for z in range(8):
            for c in range(2):
                for x in range(4):
                    pairs.append((device(y, z, c, x), device(*move(y, z, c, x))))
    return pairs


def step_x(parity):
    return pairs_of(lambda y, z, c, x: (y, z, c, x + (1 if (x + c + parity) % 2 == 0 else -1)))


def step_z(parity):
    return pairs_of(lambda y, z, c, x: (y, z + (1 if (z + c + parity) % 2 == 0 else -1), c, x))


def step_y(count):
    return pairs_of(lambda y, z, c, x: (y + count, z, c, x))


def step_near(mask):
    return pairs_of(lambda y, z, c, x: (y, z ^ mask, c, x))


SWAP = pairs_of(lambda y, z, c, x: (y, z, 1 - c, x))


ORDER = (0, 1, -1, -2, 2, 3, -3, -4)


def join(first, second):
    return jnp.concatenate([first, second], 0)


def tie(value, *others):
    return lax.optimization_barrier((value, *others))[0]


def permute(value, pairs, name):
    with jax.named_scope(name):
        return lax.ppermute(value, ALL, pairs)


def here():
    depth = lax.axis_index("high") * 4 + lax.axis_index("deep")
    return lax.axis_index("row"), depth, lax.axis_index("core"), lax.axis_index("panel")


def turn(place, core):
    return 1 - 2 * ((place + core) & 1)


def third_rows(z, c, x):
    panels = [(x + turn(x, c) * step & 3) + c * 4 for step in (0, 1, -1, -2)]
    depths = [(z + turn(z, c) * step & 7) * 8 for step in ORDER]
    return [depth + panel for panel in panels for depth in depths]


def top_rows(z, c, x):
    panels = [(x + turn(x, c) * step & 3) + c * 4 for step in (0, 1, -1, -2)]
    depths = [(z + turn(z, c) * step & 7) * 8 for step in ORDER]
    return [depth + panel for depth in depths for panel in panels]


def split(value):
    high = value.astype(jnp.bfloat16)
    return high, (value - high.astype(F32)).astype(jnp.bfloat16)


def dot(left, right):
    return jnp.dot(left, right, preferred_element_type=F32)


def split_dot(left, right):
    rows = left.shape[0]
    left_high, left_low = split(left)
    right_high, right_low = split(right)
    both = dot(jnp.concatenate([left_high, left_low], 0), right_high)
    return both[:rows] + both[rows:] + dot(left_high, right_low)


def place(pieces, width):
    rows = pieces[0][0].shape[0]
    lane = lax.broadcasted_iota(jnp.int32, (rows, 128), 1)
    pieces = sorted(pieces, key=lambda piece: piece[3])
    tiles = []
    for low in range(0, width, 128):
        total = jnp.zeros((rows, 128), F32)
        for value, source, length, target in pieces:
            if target + length <= low or target >= low + 128:
                continue
            shift = (target - source) % 128
            moved = pltpu.roll(value, shift, 1) if shift else value
            total = moved if target <= low else jnp.where(lane >= target - low, moved, total)
        tiles.append(total)
    return jnp.concatenate(tiles, 1)


def pack_kernel(d2, b2, b3, d3, d1, b1, d0, y_out, h_out, b_out, h2, g2, g3, h3, h1, g1, h0, rows, sems):
    copies = [
        pltpu.make_async_copy(source, target, sems.at[index])
        for index, (source, target) in enumerate(
            [(d1, h1), (b1, g1), (d0, h0), (d2, h2), (b2, g2), (b3, g3), (d3, h3)]
        )
    ]
    for copy in copies:
        copy.start()
    rows[...] = jnp.zeros(rows.shape, F32)
    b_out[...] = jnp.zeros(b_out.shape, F32)
    for copy in copies:
        copy.wait()
    rows[0:20, 0:Q] = h1[...]
    rows[20:40, 0:Q] = g1[...]
    rows[40:50, 0:Q] = h0[...]
    y_out[...] = rows[...].T[:Q]
    rows[0:40, 0:Q] = h2[...]
    rows[40:120, 0:Q] = g2[...]
    h_out[...] = rows[...].T[:Q]
    b_out[0:Q, :] = g3[:, 0:128]
    b_out[Q : 2 * Q, 0:112] = g3[:, 128:240]
    rows[0:80, 0:Q] = h3[...]
    rows[80:128, :] = jnp.zeros((48, 256), F32)
    turned = rows[...].T[:Q]
    for panel in range(4):
        for half in range(2):
            target = 2 * Q + panel * 40 + half * 20
            source = half * 80 + panel * 20
            b_out[target : target + 20, :] = turned[source : source + 20]


def merge_kernel(own, one, two, three, out):
    lane = lax.broadcasted_iota(jnp.int32, (Q, 128), 1)
    is_odd = here()[0] & 1 == 1
    lower = jnp.where(is_odd, one[...], own[...])
    upper = jnp.where(is_odd, own[...], three[...])
    total = jnp.zeros((Q, 128), F32)
    for value, shift, start, stop in (
        (lower, 0, 0, 20),
        (upper, 20, 20, 40),
        (lower, 20, 40, 60),
        (upper, 40, 60, 80),
        (own[...], 40, 80, 90),
        (one[...], 50, 90, 100),
        (two[...], 60, 100, 110),
        (three[...], 70, 110, 120),
    ):
        moved = pltpu.roll(value, shift, 1) if shift else value
        total = jnp.where((lane >= start) & (lane < stop), moved, total)
    out[...] = total


def b_panels():
    _, _, c, x = here()
    return [x + turn(x, c) * ORDER[slot] & 3 for slot in range(4)]


def run(copies, sems):
    copies = [
        pltpu.make_async_copy(source, target, sems.at[index])
        for index, (source, target) in enumerate(copies)
    ]
    for copy in copies:
        copy.start()
    for copy in copies:
        copy.wait()


def pick_kernel(pair, last, out, picked, sems):
    _, _, _, x = here()
    copies = []
    for slot, panel in enumerate(b_panels()):
        source = pair if slot < 2 else last
        start = pl.multiple_of(slot % 2 * 3 * Q + 2 * Q + x * 40, 8)
        target = pl.multiple_of(panel * 40, 8)
        copies.append((source.at[pl.ds(start, 40), :], picked.at[pl.ds(target, 40), :]))
    run(copies, sems)
    lane = lax.broadcasted_iota(jnp.int32, (80, 128), 1)
    out[0:80, :] = jnp.where(lane < 64, picked[0:80, :], pltpu.roll(picked[80:160, :], 64, 1))
    lane = lax.broadcasted_iota(jnp.int32, (20, 128), 1)
    total = jnp.zeros((20, 128), F32)
    for part in range(8):
        value = picked[part * 20 : part * 20 + 20, :]
        moved = pltpu.roll(value, (part * 16 - 64) % 128, 1)
        total = moved if part == 0 else jnp.where(lane >= part * 16, moved, total)
    out[80:104, :] = jnp.concatenate([total, jnp.zeros((4, 128), F32)], 0)


def unpick(packed):
    lane = lax.broadcasted_iota(jnp.int32, (Q, 128), 1)
    main, rest = packed[0:80, :], packed[80:100, :]
    main = jnp.concatenate([main, pltpu.roll(main, 64, 1)], 0)
    rest = jnp.concatenate(
        [pltpu.roll(rest, (64 - part * 16) % 128, 1) for part in range(8)], 0
    )
    return jnp.where(lane < 64, main, jnp.where(lane < 80, rest, 0.0))


def bottom_kernel(near, near_other, pair, last, out, below, inverse, sems):
    _, z, c, x = here()
    copies = []
    for slot, panel in enumerate(b_panels()):
        source = pair if slot < 2 else last
        column = pl.multiple_of(panel * Q, Q)
        for half in range(2):
            start = slot % 2 * 3 * Q + half * Q
            copies.append((source.at[pl.ds(start, Q), :], below.at[half, pl.ds(column, Q), :]))
    for core, source in enumerate((near, near_other)):
        for slot in range(4):
            lane = (z & 3 ^ slot) * 2 + (c ^ core)
            copies.append((source.at[pl.ds(slot * 104, 104), :], inverse.at[lane]))
    run(copies, sems)
    squares = jnp.zeros((Q, 128), F32)
    mixed = jnp.zeros((Q, 256), F32)
    for lane in range(8):
        part = unpick(inverse[lane])
        squares = squares + part * part
        rows = slice(lane * 80, lane * 80 + 80)
        mixed = mixed + split_dot(
            part[:, :80], jnp.concatenate([below[0, rows, :], below[1, rows, :]], 1)
        )
    squares = jnp.sum(squares, 1, keepdims=True)
    lane = lax.broadcasted_iota(jnp.int32, (Q, 256), 1)
    mixed = jnp.where(lane == 240, squares, mixed)
    out[...] = jnp.zeros(out.shape, F32)
    for part in range(8):
        out[part, 0:20, :] = mixed[part * 20 : part * 20 + 20]


def start_copies(sources, stage, sems):
    copies = [
        pltpu.make_async_copy(source, stage.at[index], sems.at[index])
        for index, source in enumerate(sources)
    ]
    for copy in copies:
        copy.start()
    return copies


def split_stage(copies, blocks, stage, high, low):
    for index, copy in enumerate(copies):
        copy.wait()
        for atom in range(8):
            number = blocks[index * 8 + atom]
            rows = pl.ds(pl.multiple_of((number & 3) * Q, Q), Q)
            first, second = split(stage[index, atom * Q : atom * Q + Q, :])
            high[number >> 2, rows, :] = first
            low[number >> 2, rows, :] = second


def leaf_pair(ref, z):
    return jnp.concatenate([ref[2 * z], ref[2 * z + 1]], 1)


def halves(left):
    left_high, left_low = split(left)
    return left_high, jnp.concatenate([left_high, left_low], 0)


def half_dot(left, high, low):
    left_high, left_both = left
    rows = left_high.shape[0]
    both = dot(left_both, high)
    return both[:rows] + both[rows:] + dot(left_high, low)


def one_hot(rows, count, base):
    row = lax.broadcasted_iota(jnp.int32, (rows, W), 0)
    lane = lax.broadcasted_iota(jnp.int32, (rows, W), 1)
    return jnp.where((row < count) & (lane == base + row), 1.0, 0.0).astype(F32)


def chain_kernel(mixed, *refs):
    first, second, t_last, h_last = refs[8:12]
    h_parts = [(first, 1), (second, 1), (second, 2), (h_last, 0)]
    t_parts = [(first, 0), (first, 2), (second, 0), (t_last, 0)]
    rows = 8 * Q
    third = refs[:4] + tuple(swap.at[pl.ds(part * rows, rows), :] for swap, part in h_parts)
    top = refs[4:8] + tuple(swap.at[pl.ds(part * rows, rows), :] for swap, part in t_parts)
    out, third_stage, top_stage, high, low, third_sems, top_sems = refs[12:]
    y, z, c, x = here()
    leaf = z * 2 + c
    third_copies = start_copies(third, third_stage, third_sems)
    top_copies = start_copies(top, top_stage, top_sems)
    third_blocks = third_rows(z, c, x) + third_rows(z, 1 - c, x)
    top_blocks = top_rows(z, c, x) + top_rows(z, 1 - c, x)
    pieces = []
    for part in range(8):
        pieces.append((mixed[part, :, 0:128], 0, 128, part * 240))
        pieces.append((mixed[part, :, 128:256], 0, 112, part * 240 + 128))
    path = place(pieces, 3 * W)
    squares = jnp.concatenate([mixed[0, :, 240:241], jnp.zeros((40, 1), F32)], 0)

    def products(cols):
        left = halves(cols)
        for z in range(8):
            product = half_dot(left, leaf_pair(high, z), leaf_pair(low, z))
            for core in range(2):
                yield z, core, product[:, core * 128 : core * 128 + 128]

    split_stage(third_copies, third_blocks, third_stage, high, low)
    cols = jnp.concatenate([path[:, 2 * W :], one_hot(16, 10, leaf * 40 + x * 10)], 0)
    pieces = [(part, 0, 40, z * 80 + core * 40) for z, core, part in products(cols)]
    cols = place(pieces, W)
    squares = squares + jnp.concatenate(
        [jnp.sum(cols * cols, 1, keepdims=True), jnp.zeros((24, 1), F32)], 0
    )
    pieces = [(part, 40, 80, z * 160 + core * 80) for z, core, part in products(cols)]
    change = place(pieces, 2 * W)
    path = jnp.concatenate([path[:, : 2 * W] - change[0:24], -change[24:40]], 0)

    split_stage(top_copies, top_blocks, top_stage, high, low)
    cols = jnp.concatenate([path[:, W:], one_hot(8, 5, ((y & 1) * 16 + leaf) * 20 + x * 5)], 0)
    pieces = [
        (part, half * 20, 20, half * 320 + z * 40 + core * 20)
        for z, core, part in products(cols)
        for half in range(2)
    ]
    cols = place(pieces, W)
    squares = squares + jnp.concatenate(
        [jnp.sum(cols * cols, 1, keepdims=True), jnp.zeros((16, 1), F32)], 0
    )
    pieces = [
        (part, 40 + half * 20, 20, half * 320 + z * 40 + core * 20)
        for z, core, part in products(cols)
        for half in range(2)
    ]
    change = place(pieces, W)
    cols = jnp.concatenate(
        [path[:, :W] - change[0:40], -change[40:48], one_hot(16, 10, (y * 16 + leaf) * 10)], 0
    )
    lane = lax.broadcasted_iota(jnp.int32, (64, 128), 1)
    total = jnp.zeros((64, 128), F32)
    for _, _, part in products(cols):
        total = total + part * part
    total = jnp.where((lane >= 80) & (lane < 120), total, 0.0)
    squares = squares + jnp.sum(total, 1, keepdims=True)
    square = jnp.concatenate(
        [jnp.broadcast_to(squares, (64, 128)), jnp.zeros((64, 128), F32)], 0
    )
    out[...] = square.T[0:1, :]


def finish_kernel(own, gathered, *outs):
    for out, start, count in zip(outs, (48, 40, 24, 0), (10, 5, 10, 20)):
        if start == 48:
            out[...] = own[0:1, start : start + count]
            continue
        parts = []
        for panel in range(4):
            row = jnp.broadcast_to(gathered[panel : panel + 1, :], (8, 128))
            parts.append((row, start, count, panel * count))
        out[...] = place(parts, 128)[0:1, : 4 * count]


def call(kernel, out_shapes, in_specs, scratch=(), limit=24):
    shapes = [jax.ShapeDtypeStruct(shape, F32) for shape in out_shapes]
    return pl.pallas_call(
        kernel,
        out_shape=shapes,
        in_specs=in_specs,
        out_specs=[VMEM] * len(shapes),
        scratch_shapes=list(scratch),
        compiler_params=pltpu.CompilerParams(vmem_limit_bytes=limit * 2**20),
        cost_estimate=pl.CostEstimate(flops=0, bytes_accessed=0, transcendentals=0),
    )


def shards(d0, d1, d2, d3, b1, b2, b3):
    b3 = b3.T
    y_chunk, h_chunk, b_chunk = call(
        pack_kernel,
        [(Q, 128), (Q, 128), (3 * Q, 128)],
        [HBM] * 7,
        [pltpu.VMEM(value.shape, F32) for value in (d2, b2, b3, d3, d1, b1, d0)]
        + [pltpu.VMEM((128, 256), F32), pltpu.SemaphoreType.DMA((7,))],
        limit=60,
    )(d2, b2, b3, d3, d1, b1, d0)

    def send(name, pairs, value):
        return permute(value, pairs, name)

    def together(*values):
        return lax.optimization_barrier(values)

    y1 = send("y1", step_y(1), y_chunk)
    y3 = send("y3", step_y(3), y_chunk)
    y2 = send("y2", step_y(2), y_chunk)
    hz = send("hz0", step_z(0), h_chunk)
    bx = send("bx0", step_x(0), b_chunk)
    y1, y2, y3, hz, bx = together(y1, y2, y3, hz, bx)
    (t_chunk,) = call(merge_kernel, [(Q, 128)], [VMEM] * 4)(y_chunk, y1, y2, y3)
    h_pair, b_pair = join(h_chunk, hz), join(b_chunk, bx)
    t_chunk, h_pair, b_pair = together(t_chunk, h_pair, b_pair)

    tx = send("tx0", step_x(0), t_chunk)
    h1 = send("hz1", step_z(1), h_pair)
    b_last = send("bx1", step_x(1), b_pair)
    tx, h1, b_last = together(tx, h1, b_last)
    t_pair = join(t_chunk, tx)
    (near,) = call(
        pick_kernel,
        [(104, 128)],
        [HBM] * 2,
        [pltpu.VMEM((Q, 128), F32), pltpu.SemaphoreType.DMA((4,))],
    )(b_pair, b_last)
    t_pair, h1, near = together(t_pair, h1, near)

    tx = send("tx1", step_x(1), t_pair)
    h2 = send("hz2", step_z(0), h1)
    got = send("near1", step_near(1), near)
    tx, h2, got = together(tx, h2, got)
    t_line, near = join(t_pair, tx), join(near, got)
    t_line, near, h2 = together(t_line, near, h2)

    tz = send("tz0", step_z(0), t_line)
    h3 = send("hz3", step_z(1), h2)
    got = send("near2", step_near(2), near)
    tz, h3, got = together(tz, h3, got)
    t0, near = join(t_line, tz), join(near, got)
    h_rows = jnp.concatenate([h_pair, h1, h2, h3], 0)
    t0, h_rows, near = together(t0, h_rows, near)

    t1 = send("tz1", step_z(1), t0)
    hx = send("hx0", step_x(0), h_rows)
    near_other = send("near_swap", SWAP, near)
    t1, hx, near_other, h_rows, t0 = together(t1, hx, near_other, h_rows, t0)

    t2 = send("tz2", step_z(0), t1)
    h1 = send("hx1", step_x(1), h_rows)
    swap1 = send("swap1", SWAP, jnp.concatenate([t0, h_rows, t1], 0))
    (mixed,) = call(
        bottom_kernel,
        [(8, 24, 256)],
        [HBM] * 4,
        [
            pltpu.VMEM((2, W, 128), F32),
            pltpu.VMEM((8, 104, 128), F32),
            pltpu.SemaphoreType.DMA((16,)),
        ],
    )(near, near_other, b_pair, b_last)
    t2, h1, swap1, mixed, hx = together(t2, h1, swap1, mixed, hx)

    t3 = send("tz3", step_z(1), t2)
    h2 = send("hx2", step_x(1), hx)
    swap2 = send("swap2", SWAP, jnp.concatenate([t2, hx, h1], 0))
    mixed = lax.all_to_all(mixed, ("deep", "core"), 0, 0, tiled=True)
    t3, h2, mixed, swap2 = together(t3, h2, mixed, swap2)

    u3 = send("swap_t3", SWAP, t3)
    g2 = send("swap_h2", SWAP, h2)

    (variances,) = call(
        chain_kernel,
        [(1, 128)],
        [VMEM] + [HBM] * 12,
        [
            pltpu.VMEM((8, 8 * Q, 128), F32),
            pltpu.VMEM((8, 8 * Q, 128), F32),
            pltpu.VMEM((16, W, 128), jnp.bfloat16),
            pltpu.VMEM((16, W, 128), jnp.bfloat16),
            pltpu.SemaphoreType.DMA((8,)),
            pltpu.SemaphoreType.DMA((8,)),
        ],
        limit=60,
    )(mixed, h_rows, hx, h1, h2, t0, t1, t2, t3, swap1, swap2, u3, g2)
    gathered = lax.all_gather(variances, "panel", axis=0, tiled=True)
    outs = call(finish_kernel, [(1, 10), (1, 20), (1, 40), (1, 80)], [VMEM] * 2)(
        variances, gathered
    )
    return tuple(out.reshape(out.shape[1]) for out in outs)


def solution(mesh):
    fine = Mesh(mesh.devices.reshape(4, 2, 4, 2, 4), ALL)
    rows = ALL[:4]
    return jax.shard_map(
        shards,
        mesh=fine,
        in_specs=(P(rows, "panel"),) * 7,
        out_specs=(P(rows),) * 4,
        check_vma=False,
    )
```

```python
import jax
import jax.numpy as jnp
from jax import lax
from jax.experimental import pallas as pl
from jax.experimental.pallas import tpu as pltpu
from jax.sharding import Mesh
from jax.sharding import PartitionSpec as P

W = 640
Q = 160
ALL = ("row", "high", "deep", "core", "panel")
F32 = jnp.float32
VMEM = pl.BlockSpec(memory_space=pltpu.VMEM)
HBM = pl.BlockSpec(memory_space=pl.ANY)


def device(y, z, c, x):
    return ((y % 4 * 8 + z % 8) * 2 + c) * 4 + x % 4


def pairs_of(move):
    pairs = []
    for y in range(4):
        for z in range(8):
            for c in range(2):
                for x in range(4):
                    pairs.append((device(y, z, c, x), device(*move(y, z, c, x))))
    return pairs


def step_x(parity):
    return pairs_of(lambda y, z, c, x: (y, z, c, x + (1 if (x + c + parity) % 2 == 0 else -1)))


def step_z(parity):
    return pairs_of(lambda y, z, c, x: (y, z + (1 if (z + c + parity) % 2 == 0 else -1), c, x))


def step_y(count):
    return pairs_of(lambda y, z, c, x: (y + count, z, c, x))


def step_near(mask):
    return pairs_of(lambda y, z, c, x: (y, z ^ mask, c, x))


SWAP = pairs_of(lambda y, z, c, x: (y, z, 1 - c, x))


ORDER = (0, 1, -1, -2, 2, 3, -3, -4)


def join(first, second):
    return jnp.concatenate([first, second], 0)


def tie(value, *others):
    return lax.optimization_barrier((value, *others))[0]


def permute(value, pairs, name):
    with jax.named_scope(name):
        return lax.ppermute(value, ALL, pairs)


def here():
    depth = lax.axis_index("high") * 4 + lax.axis_index("deep")
    return lax.axis_index("row"), depth, lax.axis_index("core"), lax.axis_index("panel")


def turn(place, core):
    return 1 - 2 * ((place + core) & 1)


def third_rows(z, c, x):
    panels = [(x + turn(x, c) * step & 3) + c * 4 for step in (0, 1, -1, -2)]
    depths = [(z + turn(z, c) * step & 7) * 8 for step in ORDER]
    return [depth + panel for panel in panels for depth in depths]


def top_rows(z, c, x):
    panels = [(x + turn(x, c) * step & 3) + c * 4 for step in (0, 1, -1, -2)]
    depths = [(z + turn(z, c) * step & 7) * 8 for step in ORDER]
    return [depth + panel for depth in depths for panel in panels]


def split(value):
    high = value.astype(jnp.bfloat16)
    return high, (value - high.astype(F32)).astype(jnp.bfloat16)


def dot(left, right):
    return jnp.dot(left, right, preferred_element_type=F32)


def split_dot(left, right):
    rows = left.shape[0]
    left_high, left_low = split(left)
    right_high, right_low = split(right)
    both = dot(jnp.concatenate([left_high, left_low], 0), right_high)
    return both[:rows] + both[rows:] + dot(left_high, right_low)


def place(pieces, width):
    rows = pieces[0][0].shape[0]
    lane = lax.broadcasted_iota(jnp.int32, (rows, 128), 1)
    pieces = sorted(pieces, key=lambda piece: piece[3])
    tiles = []
    for low in range(0, width, 128):
        total = jnp.zeros((rows, 128), F32)
        for value, source, length, target in pieces:
            if target + length <= low or target >= low + 128:
                continue
            shift = (target - source) % 128
            moved = pltpu.roll(value, shift, 1) if shift else value
            total = moved if target <= low else jnp.where(lane >= target - low, moved, total)
        tiles.append(total)
    return jnp.concatenate(tiles, 1)


def pack_kernel(d2, b2, b3, d3, d1, b1, d0, y_out, h_out, b_out, h2, g2, g3, h3, h1, g1, h0, rows, sems):
    copies = [
        pltpu.make_async_copy(source, target, sems.at[index])
        for index, (source, target) in enumerate(
            [(d1, h1), (b1, g1), (d0, h0), (d2, h2), (b2, g2), (b3, g3), (d3, h3)]
        )
    ]
    for copy in copies:
        copy.start()
    rows[...] = jnp.zeros(rows.shape, F32)
    b_out[...] = jnp.zeros(b_out.shape, F32)
    for copy in copies:
        copy.wait()
    rows[0:20, 0:Q] = h1[...]
    rows[20:40, 0:Q] = g1[...]
    rows[40:50, 0:Q] = h0[...]
    y_out[...] = rows[...].T[:Q]
    rows[0:40, 0:Q] = h2[...]
    rows[40:120, 0:Q] = g2[...]
    h_out[...] = rows[...].T[:Q]
    b_out[0:Q, :] = g3[:, 0:128]
    b_out[Q : 2 * Q, 0:112] = g3[:, 128:240]
    rows[0:80, 0:Q] = h3[...]
    rows[80:128, :] = jnp.zeros((48, 256), F32)
    turned = rows[...].T[:Q]
    for panel in range(4):
        for half in range(2):
            target = 2 * Q + panel * 40 + half * 20
            source = half * 80 + panel * 20
            b_out[target : target + 20, :] = turned[source : source + 20]


def merge_kernel(own, one, two, three, out):
    lane = lax.broadcasted_iota(jnp.int32, (Q, 128), 1)
    is_odd = here()[0] & 1 == 1
    lower = jnp.where(is_odd, one[...], own[...])
    upper = jnp.where(is_odd, own[...], three[...])
    total = jnp.zeros((Q, 128), F32)
    for value, shift, start, stop in (
        (lower, 0, 0, 20),
        (upper, 20, 20, 40),
        (lower, 20, 40, 60),
        (upper, 40, 60, 80),
        (own[...], 40, 80, 90),
        (one[...], 50, 90, 100),
        (two[...], 60, 100, 110),
        (three[...], 70, 110, 120),
    ):
        moved = pltpu.roll(value, shift, 1) if shift else value
        total = jnp.where((lane >= start) & (lane < stop), moved, total)
    out[...] = total


def b_panels():
    _, _, c, x = here()
    return [x + turn(x, c) * ORDER[slot] & 3 for slot in range(4)]


def run(copies, sems):
    copies = [
        pltpu.make_async_copy(source, target, sems.at[index])
        for index, (source, target) in enumerate(copies)
    ]
    for copy in copies:
        copy.start()
    for copy in copies:
        copy.wait()


def pick_kernel(pair, last, out, picked, sems):
    _, _, _, x = here()
    copies = []
    for slot, panel in enumerate(b_panels()):
        source = pair if slot < 2 else last
        start = pl.multiple_of(slot % 2 * 3 * Q + 2 * Q + x * 40, 8)
        target = pl.multiple_of(panel * 40, 8)
        copies.append((source.at[pl.ds(start, 40), :], picked.at[pl.ds(target, 40), :]))
    run(copies, sems)
    lane = lax.broadcasted_iota(jnp.int32, (80, 128), 1)
    out[0:80, :] = jnp.where(lane < 64, picked[0:80, :], pltpu.roll(picked[80:160, :], 64, 1))
    lane = lax.broadcasted_iota(jnp.int32, (20, 128), 1)
    total = jnp.zeros((20, 128), F32)
    for part in range(8):
        value = picked[part * 20 : part * 20 + 20, :]
        moved = pltpu.roll(value, (part * 16 - 64) % 128, 1)
        total = moved if part == 0 else jnp.where(lane >= part * 16, moved, total)
    out[80:104, :] = jnp.concatenate([total, jnp.zeros((4, 128), F32)], 0)


def unpick(packed):
    lane = lax.broadcasted_iota(jnp.int32, (Q, 128), 1)
    main, rest = packed[0:80, :], packed[80:100, :]
    main = jnp.concatenate([main, pltpu.roll(main, 64, 1)], 0)
    rest = jnp.concatenate(
        [pltpu.roll(rest, (64 - part * 16) % 128, 1) for part in range(8)], 0
    )
    return jnp.where(lane < 64, main, jnp.where(lane < 80, rest, 0.0))


def bottom_kernel(near, other_one, other_two, pair, last, out, below, inverse, sems):
    _, z, c, x = here()
    copies = []
    for slot, panel in enumerate(b_panels()):
        source = pair if slot < 2 else last
        column = pl.multiple_of(panel * Q, Q)
        for half in range(2):
            start = slot % 2 * 3 * Q + half * Q
            copies.append((source.at[pl.ds(start, Q), :], below.at[half, pl.ds(column, Q), :]))
    for slot in range(4):
        lane = (z & 3 ^ slot) * 2
        other = other_one if slot < 2 else other_two
        copies.append((near.at[pl.ds(slot * 104, 104), :], inverse.at[lane + c]))
        copies.append((other.at[pl.ds(slot % 2 * 104, 104), :], inverse.at[lane + 1 - c]))
    run(copies, sems)
    squares = jnp.zeros((Q, 128), F32)
    mixed = jnp.zeros((Q, 256), F32)
    for lane in range(8):
        part = unpick(inverse[lane])
        squares = squares + part * part
        rows = slice(lane * 80, lane * 80 + 80)
        mixed = mixed + split_dot(
            part[:, :80], jnp.concatenate([below[0, rows, :], below[1, rows, :]], 1)
        )
    squares = jnp.sum(squares, 1, keepdims=True)
    lane = lax.broadcasted_iota(jnp.int32, (Q, 256), 1)
    mixed = jnp.where(lane == 240, squares, mixed)
    for part in range(8):
        rows = slice(part * 20, part * 20 + 20)
        out[part, 0:20, :] = mixed[rows, 0:128]
        out[part, 20:40, :] = mixed[rows, 128:256]


def start_copies(sources, stage, sems):
    copies = [
        pltpu.make_async_copy(source, stage.at[index], sems.at[index])
        for index, source in enumerate(sources)
    ]
    for copy in copies:
        copy.start()
    return copies


def split_stage(copies, blocks, stage, high, low):
    for index, copy in enumerate(copies):
        copy.wait()
        for atom in range(8):
            number = blocks[index * 8 + atom]
            rows = pl.ds(pl.multiple_of((number & 3) * Q, Q), Q)
            first, second = split(stage[index, atom * Q : atom * Q + Q, :])
            high[number >> 2, rows, :] = first
            low[number >> 2, rows, :] = second


def leaf_pair(ref, z):
    return jnp.concatenate([ref[2 * z], ref[2 * z + 1]], 1)


def halves(left):
    left_high, left_low = split(left)
    return left_high, jnp.concatenate([left_high, left_low], 0)


def half_dot(left, high, low):
    left_high, left_both = left
    rows = left_high.shape[0]
    both = dot(left_both, high)
    return both[:rows] + both[rows:] + dot(left_high, low)


def one_hot(rows, count, base):
    row = lax.broadcasted_iota(jnp.int32, (rows, W), 0)
    lane = lax.broadcasted_iota(jnp.int32, (rows, W), 1)
    return jnp.where((row < count) & (lane == base + row), 1.0, 0.0).astype(F32)


def chain_kernel(mixed, *refs):
    first, second, t_last, h_last = refs[8:12]
    h_parts = [(first, 1), (second, 1), (second, 2), (h_last, 0)]
    t_parts = [(first, 0), (first, 2), (second, 0), (t_last, 0)]
    rows = 8 * Q
    third = refs[:4] + tuple(swap.at[pl.ds(part * rows, rows), :] for swap, part in h_parts)
    top = refs[4:8] + tuple(swap.at[pl.ds(part * rows, rows), :] for swap, part in t_parts)
    out, third_stage, top_stage, high, low, third_sems, top_sems = refs[12:]
    y, z, c, x = here()
    leaf = z * 2 + c
    third_copies = start_copies(third, third_stage, third_sems)
    top_copies = start_copies(top, top_stage, top_sems)
    third_blocks = third_rows(z, c, x) + third_rows(z, 1 - c, x)
    top_blocks = top_rows(z, c, x) + top_rows(z, 1 - c, x)
    pieces = []
    for part in range(8):
        tail = jnp.concatenate([mixed[part, 20:40, :], jnp.zeros((4, 128), F32)], 0)
        pieces.append((mixed[part, 0:24, :], 0, 128, part * 240))
        pieces.append((tail, 0, 112, part * 240 + 128))
    path = place(pieces, 3 * W)
    squares = jnp.concatenate([mixed[0, 20:40, 112:113], jnp.zeros((44, 1), F32)], 0)

    def products(cols):
        left = halves(cols)
        for z in range(8):
            product = half_dot(left, leaf_pair(high, z), leaf_pair(low, z))
            for core in range(2):
                yield z, core, product[:, core * 128 : core * 128 + 128]

    split_stage(third_copies, third_blocks, third_stage, high, low)
    cols = jnp.concatenate([path[:, 2 * W :], one_hot(16, 10, leaf * 40 + x * 10)], 0)
    pieces = [(part, 0, 40, z * 80 + core * 40) for z, core, part in products(cols)]
    cols = place(pieces, W)
    squares = squares + jnp.concatenate(
        [jnp.sum(cols * cols, 1, keepdims=True), jnp.zeros((24, 1), F32)], 0
    )
    pieces = [(part, 40, 80, z * 160 + core * 80) for z, core, part in products(cols)]
    change = place(pieces, 2 * W)
    path = jnp.concatenate([path[:, : 2 * W] - change[0:24], -change[24:40]], 0)

    split_stage(top_copies, top_blocks, top_stage, high, low)
    cols = jnp.concatenate([path[:, W:], one_hot(8, 5, ((y & 1) * 16 + leaf) * 20 + x * 5)], 0)
    pieces = [
        (part, half * 20, 20, half * 320 + z * 40 + core * 20)
        for z, core, part in products(cols)
        for half in range(2)
    ]
    cols = place(pieces, W)
    squares = squares + jnp.concatenate(
        [jnp.sum(cols * cols, 1, keepdims=True), jnp.zeros((16, 1), F32)], 0
    )
    pieces = [
        (part, 40 + half * 20, 20, half * 320 + z * 40 + core * 20)
        for z, core, part in products(cols)
        for half in range(2)
    ]
    change = place(pieces, W)
    cols = jnp.concatenate(
        [path[:, :W] - change[0:40], -change[40:48], one_hot(16, 10, (y * 16 + leaf) * 10)], 0
    )
    lane = lax.broadcasted_iota(jnp.int32, (64, 128), 1)
    total = jnp.zeros((64, 128), F32)
    for _, _, part in products(cols):
        total = total + part * part
    total = jnp.where((lane >= 80) & (lane < 120), total, 0.0)
    squares = squares + jnp.sum(total, 1, keepdims=True)
    square = jnp.concatenate(
        [jnp.broadcast_to(squares, (64, 128)), jnp.zeros((64, 128), F32)], 0
    )
    out[...] = square.T[0:1, :]


def finish_kernel(own, gathered, *outs):
    for out, start, count in zip(outs, (48, 40, 24, 0), (10, 5, 10, 20)):
        if start == 48:
            out[...] = own[0:1, start : start + count]
            continue
        parts = []
        for panel in range(4):
            row = jnp.broadcast_to(gathered[panel : panel + 1, :], (8, 128))
            parts.append((row, start, count, panel * count))
        out[...] = place(parts, 128)[0:1, : 4 * count]


def call(kernel, out_shapes, in_specs, scratch=(), limit=24):
    shapes = [jax.ShapeDtypeStruct(shape, F32) for shape in out_shapes]
    return pl.pallas_call(
        kernel,
        out_shape=shapes,
        in_specs=in_specs,
        out_specs=[VMEM] * len(shapes),
        scratch_shapes=list(scratch),
        compiler_params=pltpu.CompilerParams(vmem_limit_bytes=limit * 2**20),
        cost_estimate=pl.CostEstimate(flops=0, bytes_accessed=0, transcendentals=0),
    )


def shards(d0, d1, d2, d3, b1, b2, b3):
    b3 = b3.T
    y_chunk, h_chunk, b_chunk = call(
        pack_kernel,
        [(Q, 128), (Q, 128), (3 * Q, 128)],
        [HBM] * 7,
        [pltpu.VMEM(value.shape, F32) for value in (d2, b2, b3, d3, d1, b1, d0)]
        + [pltpu.VMEM((128, 256), F32), pltpu.SemaphoreType.DMA((7,))],
        limit=60,
    )(d2, b2, b3, d3, d1, b1, d0)

    def send(name, pairs, value):
        return permute(value, pairs, name)

    def together(*values):
        return lax.optimization_barrier(values)

    y1 = send("y1", step_y(1), y_chunk)
    y3 = send("y3", step_y(3), y_chunk)
    y2 = send("y2", step_y(2), y_chunk)
    hz = send("hz0", step_z(0), h_chunk)
    bx = send("bx0", step_x(0), b_chunk)
    (t_chunk,) = call(merge_kernel, [(Q, 128)], [VMEM] * 4)(y_chunk, y1, y2, y3)
    h_pair, b_pair = join(h_chunk, hz), tie(join(b_chunk, bx), hz, y1)

    tx = send("tx0", step_x(0), t_chunk)
    h1 = send("hz1", step_z(1), h_pair)
    b_last = send("bx1", step_x(1), b_pair)
    (near,) = call(
        pick_kernel,
        [(104, 128)],
        [HBM] * 2,
        [pltpu.VMEM((Q, 128), F32), pltpu.SemaphoreType.DMA((4,))],
    )(b_pair, b_last)
    got = send("near1", step_near(1), near)
    tx, h1, got = together(tx, h1, got)
    t_pair, near = join(t_chunk, tx), join(near, got)
    t_pair, h1, near = together(t_pair, h1, near)

    tx = send("tx1", step_x(1), t_pair)
    h2 = send("hz2", step_z(0), h1)
    got = send("near2", step_near(2), near)
    other_one = send("near_swap1", SWAP, near)
    tx, h2, got, other_one = together(tx, h2, got, other_one)
    t_line, near = join(t_pair, tx), join(near, got)
    t_line, near, got, h2 = together(t_line, near, got, h2)

    tz = send("tz0", step_z(0), t_line)
    h3 = send("hz3", step_z(1), h2)
    other_two = send("near_swap2", SWAP, got)
    tz, h3, other_two = together(tz, h3, other_two)
    t0 = join(t_line, tz)
    h_rows = jnp.concatenate([h_pair, h1, h2, h3], 0)
    t0, h_rows, other_two = together(t0, h_rows, other_two)

    t1 = send("tz1", step_z(1), t0)
    hx = send("hx0", step_x(0), h_rows)
    (mixed,) = call(
        bottom_kernel,
        [(8, 40, 128)],
        [HBM] * 5,
        [
            pltpu.VMEM((2, W, 128), F32),
            pltpu.VMEM((8, 104, 128), F32),
            pltpu.SemaphoreType.DMA((16,)),
        ],
    )(near, other_one, other_two, b_pair, b_last)
    t1, hx, mixed, h_rows, t0 = together(t1, hx, mixed, h_rows, t0)

    t2 = send("tz2", step_z(0), t1)
    h1 = send("hx1", step_x(1), h_rows)
    swap1 = send("swap1", SWAP, jnp.concatenate([t0, h_rows, t1], 0))
    mixed = lax.all_to_all(mixed, ("deep", "core"), 0, 0, tiled=True)
    t2, h1, swap1, mixed, hx = together(t2, h1, swap1, mixed, hx)

    t3 = send("tz3", step_z(1), t2)
    h2 = send("hx2", step_x(1), hx)
    swap2 = send("swap2", SWAP, jnp.concatenate([t2, hx, h1], 0))
    t3, h2, mixed, swap2 = together(t3, h2, mixed, swap2)

    u3 = send("swap_t3", SWAP, t3)
    g2 = send("swap_h2", SWAP, h2)

    (variances,) = call(
        chain_kernel,
        [(1, 128)],
        [VMEM] + [HBM] * 12,
        [
            pltpu.VMEM((8, 8 * Q, 128), F32),
            pltpu.VMEM((8, 8 * Q, 128), F32),
            pltpu.VMEM((16, W, 128), jnp.bfloat16),
            pltpu.VMEM((16, W, 128), jnp.bfloat16),
            pltpu.SemaphoreType.DMA((8,)),
            pltpu.SemaphoreType.DMA((8,)),
        ],
        limit=60,
    )(mixed, h_rows, hx, h1, h2, t0, t1, t2, t3, swap1, swap2, u3, g2)
    gathered = lax.all_gather(variances, "panel", axis=0, tiled=True)
    outs = call(finish_kernel, [(1, 10), (1, 20), (1, 40), (1, 80)], [VMEM] * 2)(
        variances, gathered
    )
    return tuple(out.reshape(out.shape[1]) for out in outs)


def solution(mesh):
    fine = Mesh(mesh.devices.reshape(4, 2, 4, 2, 4), ALL)
    rows = ALL[:4]
    return jax.shard_map(
        shards,
        mesh=fine,
        in_specs=(P(rows, "panel"),) * 7,
        out_specs=(P(rows),) * 4,
        check_vma=False,
    )
```

```python
import jax
import jax.numpy as jnp
from jax import lax
from jax.experimental import pallas as pl
from jax.experimental.pallas import tpu as pltpu
from jax.sharding import Mesh
from jax.sharding import PartitionSpec as P

W = 640
Q = 160
ALL = ("row", "high", "deep", "core", "panel")
F32 = jnp.float32
VMEM = pl.BlockSpec(memory_space=pltpu.VMEM)
HBM = pl.BlockSpec(memory_space=pl.ANY)


def device(y, z, c, x):
    return ((y % 4 * 8 + z % 8) * 2 + c) * 4 + x % 4


def pairs_of(move):
    pairs = []
    for y in range(4):
        for z in range(8):
            for c in range(2):
                for x in range(4):
                    pairs.append((device(y, z, c, x), device(*move(y, z, c, x))))
    return pairs


def step_x(parity):
    return pairs_of(lambda y, z, c, x: (y, z, c, x + (1 if (x + c + parity) % 2 == 0 else -1)))


def step_z(parity):
    return pairs_of(lambda y, z, c, x: (y, z + (1 if (z + c + parity) % 2 == 0 else -1), c, x))


def step_y(count):
    return pairs_of(lambda y, z, c, x: (y + count, z, c, x))


def step_near(mask):
    return pairs_of(lambda y, z, c, x: (y, z ^ mask, c, x))


SWAP = pairs_of(lambda y, z, c, x: (y, z, 1 - c, x))


ORDER = (0, 1, -1, -2, 2, 3, -3, -4)


def join(first, second):
    return jnp.concatenate([first, second], 0)


def tie(value, *others):
    return lax.optimization_barrier((value, *others))[0]


def permute(value, pairs, name):
    with jax.named_scope(name):
        return lax.ppermute(value, ALL, pairs)


def here():
    depth = lax.axis_index("high") * 4 + lax.axis_index("deep")
    return lax.axis_index("row"), depth, lax.axis_index("core"), lax.axis_index("panel")


def turn(place, core):
    return 1 - 2 * ((place + core) & 1)


def third_rows(z, c, x):
    panels = [(x + turn(x, c) * step & 3) + c * 4 for step in (0, 1, -1, -2)]
    depths = [(z + turn(z, c) * step & 7) * 8 for step in ORDER]
    return [depth + panel for panel in panels for depth in depths]


def top_rows(z, c, x):
    panels = [(x + turn(x, c) * step & 3) + c * 4 for step in (0, 1, -1, -2)]
    depths = [(z + turn(z, c) * step & 7) * 8 for step in ORDER]
    return [depth + panel for depth in depths for panel in panels]


def split(value):
    high = value.astype(jnp.bfloat16)
    return high, (value - high.astype(F32)).astype(jnp.bfloat16)


def dot(left, right):
    return jnp.dot(left, right, preferred_element_type=F32)


def split_dot(left, right):
    rows = left.shape[0]
    left_high, left_low = split(left)
    right_high, right_low = split(right)
    both = dot(jnp.concatenate([left_high, left_low], 0), right_high)
    return both[:rows] + both[rows:] + dot(left_high, right_low)


def place(pieces, width):
    rows = pieces[0][0].shape[0]
    lane = lax.broadcasted_iota(jnp.int32, (rows, 128), 1)
    pieces = sorted(pieces, key=lambda piece: piece[3])
    tiles = []
    for low in range(0, width, 128):
        total = jnp.zeros((rows, 128), F32)
        for value, source, length, target in pieces:
            if target + length <= low or target >= low + 128:
                continue
            shift = (target - source) % 128
            moved = pltpu.roll(value, shift, 1) if shift else value
            total = moved if target <= low else jnp.where(lane >= target - low, moved, total)
        tiles.append(total)
    return jnp.concatenate(tiles, 1)


def pack_kernel(d2, b2, b3, d3, d1, b1, d0, y_out, h_out, b_out, h2, g2, g3, h3, h1, g1, h0, rows, sems):
    copies = [
        pltpu.make_async_copy(source, target, sems.at[index])
        for index, (source, target) in enumerate(
            [(d1, h1), (b1, g1), (d0, h0), (d2, h2), (b2, g2), (b3, g3), (d3, h3)]
        )
    ]
    for copy in copies:
        copy.start()
    rows[...] = jnp.zeros(rows.shape, F32)
    b_out[...] = jnp.zeros(b_out.shape, F32)
    for copy in copies:
        copy.wait()
    rows[0:20, 0:Q] = h1[...]
    rows[20:40, 0:Q] = g1[...]
    rows[40:50, 0:Q] = h0[...]
    y_out[...] = rows[...].T[:Q]
    rows[0:40, 0:Q] = h2[...]
    rows[40:120, 0:Q] = g2[...]
    h_out[...] = rows[...].T[:Q]
    b_out[0:Q, :] = g3[:, 0:128]
    b_out[Q : 2 * Q, 0:112] = g3[:, 128:240]
    rows[0:80, 0:Q] = h3[...]
    rows[80:128, :] = jnp.zeros((48, 256), F32)
    turned = rows[...].T[:Q]
    for panel in range(4):
        for half in range(2):
            target = 2 * Q + panel * 40 + half * 20
            source = half * 80 + panel * 20
            b_out[target : target + 20, :] = turned[source : source + 20]


def merge_kernel(own, one, two, three, out):
    lane = lax.broadcasted_iota(jnp.int32, (Q, 128), 1)
    is_odd = here()[0] & 1 == 1
    lower = jnp.where(is_odd, one[...], own[...])
    upper = jnp.where(is_odd, own[...], three[...])
    total = jnp.zeros((Q, 128), F32)
    for value, shift, start, stop in (
        (lower, 0, 0, 20),
        (upper, 20, 20, 40),
        (lower, 20, 40, 60),
        (upper, 40, 60, 80),
        (own[...], 40, 80, 90),
        (one[...], 50, 90, 100),
        (two[...], 60, 100, 110),
        (three[...], 70, 110, 120),
    ):
        moved = pltpu.roll(value, shift, 1) if shift else value
        total = jnp.where((lane >= start) & (lane < stop), moved, total)
    out[...] = total


def b_panels():
    _, _, c, x = here()
    return [x + turn(x, c) * ORDER[slot] & 3 for slot in range(4)]


def run(copies, sems):
    copies = [
        pltpu.make_async_copy(source, target, sems.at[index])
        for index, (source, target) in enumerate(copies)
    ]
    for copy in copies:
        copy.start()
    for copy in copies:
        copy.wait()


def pick_kernel(pair, last, out, picked, sems):
    _, _, _, x = here()
    copies = []
    for slot, panel in enumerate(b_panels()):
        source = pair if slot < 2 else last
        start = pl.multiple_of(slot % 2 * 3 * Q + 2 * Q + x * 40, 8)
        target = pl.multiple_of(panel * 40, 8)
        copies.append((source.at[pl.ds(start, 40), :], picked.at[pl.ds(target, 40), :]))
    run(copies, sems)
    lane = lax.broadcasted_iota(jnp.int32, (80, 128), 1)
    out[0:80, :] = jnp.where(lane < 64, picked[0:80, :], pltpu.roll(picked[80:160, :], 64, 1))
    lane = lax.broadcasted_iota(jnp.int32, (20, 128), 1)
    total = jnp.zeros((20, 128), F32)
    for part in range(8):
        value = picked[part * 20 : part * 20 + 20, :]
        moved = pltpu.roll(value, (part * 16 - 64) % 128, 1)
        total = moved if part == 0 else jnp.where(lane >= part * 16, moved, total)
    out[80:104, :] = jnp.concatenate([total, jnp.zeros((4, 128), F32)], 0)


def unpick(packed):
    lane = lax.broadcasted_iota(jnp.int32, (Q, 128), 1)
    main, rest = packed[0:80, :], packed[80:100, :]
    main = jnp.concatenate([main, pltpu.roll(main, 64, 1)], 0)
    rest = jnp.concatenate(
        [pltpu.roll(rest, (64 - part * 16) % 128, 1) for part in range(8)], 0
    )
    return jnp.where(lane < 64, main, jnp.where(lane < 80, rest, 0.0))


def bottom_kernel(near, other_one, other_two, pair, last, out, below, inverse, sems):
    _, z, c, x = here()
    copies = []
    for slot, panel in enumerate(b_panels()):
        source = pair if slot < 2 else last
        column = pl.multiple_of(panel * Q, Q)
        for half in range(2):
            start = slot % 2 * 3 * Q + half * Q
            copies.append((source.at[pl.ds(start, Q), :], below.at[half, pl.ds(column, Q), :]))
    for slot in range(4):
        lane = (z & 3 ^ slot) * 2
        other = other_one if slot < 2 else other_two
        copies.append((near.at[pl.ds(slot * 104, 104), :], inverse.at[lane + c]))
        copies.append((other.at[pl.ds(slot % 2 * 104, 104), :], inverse.at[lane + 1 - c]))
    run(copies, sems)
    squares = jnp.zeros((Q, 128), F32)
    mixed = jnp.zeros((Q, 256), F32)
    for lane in range(8):
        part = unpick(inverse[lane])
        squares = squares + part * part
        rows = slice(lane * 80, lane * 80 + 80)
        mixed = mixed + split_dot(
            part[:, :80], jnp.concatenate([below[0, rows, :], below[1, rows, :]], 1)
        )
    squares = jnp.sum(squares, 1, keepdims=True)
    lane = lax.broadcasted_iota(jnp.int32, (Q, 256), 1)
    mixed = jnp.where(lane == 240, squares, mixed)
    for part in range(8):
        rows = slice(part * 20, part * 20 + 20)
        out[part, 0:20, :] = mixed[rows, 0:128]
        out[part, 20:40, :] = mixed[rows, 128:256]


def start_copies(sources, stage, sems):
    copies = [
        pltpu.make_async_copy(source, stage.at[index], sems.at[index])
        for index, source in enumerate(sources)
    ]
    for copy in copies:
        copy.start()
    return copies


def split_stage(copies, blocks, stage, high, low):
    for index, copy in enumerate(copies):
        copy.wait()
        for atom in range(8):
            number = blocks[index * 8 + atom]
            rows = pl.ds(pl.multiple_of((number & 3) * Q, Q), Q)
            first, second = split(stage[index, atom * Q : atom * Q + Q, :])
            high[number >> 2, rows, :] = first
            low[number >> 2, rows, :] = second


def leaf_pair(ref, z):
    return jnp.concatenate([ref[2 * z], ref[2 * z + 1]], 1)


def halves(left):
    left_high, left_low = split(left)
    return left_high, jnp.concatenate([left_high, left_low], 0)


def half_dot(left, high, low):
    left_high, left_both = left
    rows = left_high.shape[0]
    both = dot(left_both, high)
    return both[:rows] + both[rows:] + dot(left_high, low)


def one_hot(rows, count, base):
    row = lax.broadcasted_iota(jnp.int32, (rows, W), 0)
    lane = lax.broadcasted_iota(jnp.int32, (rows, W), 1)
    return jnp.where((row < count) & (lane == base + row), 1.0, 0.0).astype(F32)


def chain_kernel(mixed, *refs):
    first, second, t_last, h_last = refs[8:12]
    h_parts = [(first, 1), (second, 1), (second, 2), (h_last, 0)]
    t_parts = [(first, 0), (first, 2), (second, 0), (t_last, 0)]
    rows = 8 * Q
    third = refs[:4] + tuple(swap.at[pl.ds(part * rows, rows), :] for swap, part in h_parts)
    top = refs[4:8] + tuple(swap.at[pl.ds(part * rows, rows), :] for swap, part in t_parts)
    out, third_stage, top_stage, high, low, third_sems, top_sems = refs[12:]
    y, z, c, x = here()
    leaf = z * 2 + c
    third_copies = start_copies(third, third_stage, third_sems)
    top_copies = start_copies(top, top_stage, top_sems)
    third_blocks = third_rows(z, c, x) + third_rows(z, 1 - c, x)
    top_blocks = top_rows(z, c, x) + top_rows(z, 1 - c, x)
    pieces = []
    for part in range(8):
        tail = jnp.concatenate([mixed[part, 20:40, :], jnp.zeros((4, 128), F32)], 0)
        pieces.append((mixed[part, 0:24, :], 0, 128, part * 240))
        pieces.append((tail, 0, 112, part * 240 + 128))
    path = place(pieces, 3 * W)
    squares = jnp.concatenate([mixed[0, 20:40, 112:113], jnp.zeros((44, 1), F32)], 0)

    def products(cols):
        left = halves(cols)
        for z in range(8):
            product = half_dot(left, leaf_pair(high, z), leaf_pair(low, z))
            for core in range(2):
                yield z, core, product[:, core * 128 : core * 128 + 128]

    split_stage(third_copies, third_blocks, third_stage, high, low)
    cols = jnp.concatenate([path[:, 2 * W :], one_hot(16, 10, leaf * 40 + x * 10)], 0)
    pieces = [(part, 0, 40, z * 80 + core * 40) for z, core, part in products(cols)]
    cols = place(pieces, W)
    squares = squares + jnp.concatenate(
        [jnp.sum(cols * cols, 1, keepdims=True), jnp.zeros((24, 1), F32)], 0
    )
    pieces = [(part, 40, 80, z * 160 + core * 80) for z, core, part in products(cols)]
    change = place(pieces, 2 * W)
    path = jnp.concatenate([path[:, : 2 * W] - change[0:24], -change[24:40]], 0)

    split_stage(top_copies, top_blocks, top_stage, high, low)
    cols = jnp.concatenate([path[:, W:], one_hot(8, 5, ((y & 1) * 16 + leaf) * 20 + x * 5)], 0)
    pieces = [
        (part, half * 20, 20, half * 320 + z * 40 + core * 20)
        for z, core, part in products(cols)
        for half in range(2)
    ]
    cols = place(pieces, W)
    squares = squares + jnp.concatenate(
        [jnp.sum(cols * cols, 1, keepdims=True), jnp.zeros((16, 1), F32)], 0
    )
    pieces = [
        (part, 40 + half * 20, 20, half * 320 + z * 40 + core * 20)
        for z, core, part in products(cols)
        for half in range(2)
    ]
    change = place(pieces, W)
    cols = jnp.concatenate(
        [path[:, :W] - change[0:40], -change[40:48], one_hot(16, 10, (y * 16 + leaf) * 10)], 0
    )
    lane = lax.broadcasted_iota(jnp.int32, (64, 128), 1)
    total = jnp.zeros((64, 128), F32)
    for _, _, part in products(cols):
        total = total + part * part
    total = jnp.where((lane >= 80) & (lane < 120), total, 0.0)
    squares = squares + jnp.sum(total, 1, keepdims=True)
    square = jnp.concatenate(
        [jnp.broadcast_to(squares, (64, 128)), jnp.zeros((64, 128), F32)], 0
    )
    out[...] = square.T[0:1, :]


def finish_kernel(own, gathered, *outs):
    for out, start, count in zip(outs, (48, 40, 24, 0), (10, 5, 10, 20)):
        if start == 48:
            out[...] = own[0:1, start : start + count]
            continue
        parts = []
        for panel in range(4):
            row = jnp.broadcast_to(gathered[panel : panel + 1, :], (8, 128))
            parts.append((row, start, count, panel * count))
        out[...] = place(parts, 128)[0:1, : 4 * count]


def call(kernel, out_shapes, in_specs, scratch=(), limit=24):
    shapes = [jax.ShapeDtypeStruct(shape, F32) for shape in out_shapes]
    return pl.pallas_call(
        kernel,
        out_shape=shapes,
        in_specs=in_specs,
        out_specs=[VMEM] * len(shapes),
        scratch_shapes=list(scratch),
        compiler_params=pltpu.CompilerParams(vmem_limit_bytes=limit * 2**20),
        cost_estimate=pl.CostEstimate(flops=0, bytes_accessed=0, transcendentals=0),
    )


def shards(d0, d1, d2, d3, b1, b2, b3):
    b3 = b3.T
    y_chunk, h_chunk, b_chunk = call(
        pack_kernel,
        [(Q, 128), (Q, 128), (3 * Q, 128)],
        [HBM] * 7,
        [pltpu.VMEM(value.shape, F32) for value in (d2, b2, b3, d3, d1, b1, d0)]
        + [pltpu.VMEM((128, 256), F32), pltpu.SemaphoreType.DMA((7,))],
        limit=60,
    )(d2, b2, b3, d3, d1, b1, d0)

    def send(name, pairs, value):
        return permute(value, pairs, name)

    def together(*values):
        return lax.optimization_barrier(values)

    y1 = send("y1", step_y(1), y_chunk)
    y3 = send("y3", step_y(3), y_chunk)
    y2 = send("y2", step_y(2), y_chunk)
    hz = send("hz0", step_z(0), h_chunk)
    bx = send("bx0", step_x(0), b_chunk)
    (t_chunk,) = call(merge_kernel, [(Q, 128)], [VMEM] * 4)(y_chunk, y1, y2, y3)
    h_pair, b_pair = join(h_chunk, hz), tie(join(b_chunk, bx), hz, y1, y3)

    tx = send("tx0", step_x(0), t_chunk)
    h1 = send("hz1", step_z(1), h_pair)
    b_last = send("bx1", step_x(1), b_pair)
    (near,) = call(
        pick_kernel,
        [(104, 128)],
        [HBM] * 2,
        [pltpu.VMEM((Q, 128), F32), pltpu.SemaphoreType.DMA((4,))],
    )(b_pair, b_last)
    got = send("near1", step_near(1), near)
    tx, h1, got = together(tx, h1, got)
    t_pair, near = join(t_chunk, tx), join(near, got)
    t_pair, h1, near = together(t_pair, h1, near)

    tx = send("tx1", step_x(1), t_pair)
    h2 = send("hz2", step_z(0), h1)
    got = send("near2", step_near(2), near)
    other_one = send("near_swap1", SWAP, near)
    tx, h2, got, other_one = together(tx, h2, got, other_one)
    t_line, near = join(t_pair, tx), join(near, got)
    t_line, near, got, h2 = together(t_line, near, got, h2)

    tz = send("tz0", step_z(0), t_line)
    h3 = send("hz3", step_z(1), h2)
    other_two = send("near_swap2", SWAP, got)
    tz, h3, other_two = together(tz, h3, other_two)
    t0 = join(t_line, tz)
    h_rows = jnp.concatenate([h_pair, h1, h2, h3], 0)
    t0, h_rows, other_two = together(t0, h_rows, other_two)

    t1 = send("tz1", step_z(1), t0)
    hx = send("hx0", step_x(0), h_rows)
    (mixed,) = call(
        bottom_kernel,
        [(8, 40, 128)],
        [HBM] * 5,
        [
            pltpu.VMEM((2, W, 128), F32),
            pltpu.VMEM((8, 104, 128), F32),
            pltpu.SemaphoreType.DMA((16,)),
        ],
    )(near, other_one, other_two, b_pair, b_last)
    t1, hx, mixed, h_rows, t0 = together(t1, hx, mixed, h_rows, t0)

    t2 = send("tz2", step_z(0), t1)
    h1 = send("hx1", step_x(1), h_rows)
    swap1 = send("swap1", SWAP, jnp.concatenate([t0, h_rows, t1], 0))
    mixed = lax.all_to_all(mixed, ("deep", "core"), 0, 0, tiled=True)
    t2, h1, swap1, mixed, hx = together(t2, h1, swap1, mixed, hx)

    t3 = send("tz3", step_z(1), t2)
    h2 = send("hx2", step_x(1), hx)
    swap2 = send("swap2", SWAP, jnp.concatenate([t2, hx, h1], 0))
    t3, h2, mixed, swap2 = together(t3, h2, mixed, swap2)

    u3 = send("swap_t3", SWAP, t3)
    g2 = send("swap_h2", SWAP, h2)

    (variances,) = call(
        chain_kernel,
        [(1, 128)],
        [VMEM] + [HBM] * 12,
        [
            pltpu.VMEM((8, 8 * Q, 128), F32),
            pltpu.VMEM((8, 8 * Q, 128), F32),
            pltpu.VMEM((16, W, 128), jnp.bfloat16),
            pltpu.VMEM((16, W, 128), jnp.bfloat16),
            pltpu.SemaphoreType.DMA((8,)),
            pltpu.SemaphoreType.DMA((8,)),
        ],
        limit=60,
    )(mixed, h_rows, hx, h1, h2, t0, t1, t2, t3, swap1, swap2, u3, g2)
    gathered = lax.all_gather(variances, "panel", axis=0, tiled=True)
    outs = call(finish_kernel, [(1, 10), (1, 20), (1, 40), (1, 80)], [VMEM] * 2)(
        variances, gathered
    )
    return tuple(out.reshape(out.shape[1]) for out in outs)


def solution(mesh):
    fine = Mesh(mesh.devices.reshape(4, 2, 4, 2, 4), ALL)
    rows = ALL[:4]
    return jax.shard_map(
        shards,
        mesh=fine,
        in_specs=(P(rows, "panel"),) * 7,
        out_specs=(P(rows),) * 4,
        check_vma=False,
    )
```
